256 devices in a mesh: tm: 16 (over z, core), space: 16 (over y, x).
Axes of the slice: x: 4, y: 4, z: 8, core: 2. Of those that a mesh axis runs over, the one named last changes fastest.
Arguments:
- coarse_guess: float32 [32, 512, 2048], P('tm', 'space'), may hold values from -2.5 to 2.5
- initial: float32 [512, 2048], P('space'), may hold values from -2.5 to 2.5
- diffusion: float32 [512, 2048], P('space'), may hold values from 0.002 to 0.008
- velocity: float32 [2, 512, 2048], P(None, 'space'), may hold values from -0.04 to 0.04
- reaction: float32 [512, 2048], P('space'), may hold values from 0.002 to 0.006
- source: float32 [512, 2048], P('space'), may hold values from -0.2 to 0.2
Outputs:
- corrected: float32 [32, 512, 2048], P('tm', 'space')
The draws below stay inside these ranges and needn't reach their ends.
All inputs are finite; a program needn't handle non-finite values.
Results may differ from the reference program's by a relative error of at most 0.00002.
Values sent between devices are 32-bit elements; how exact they have to be, the bound alone decides.
A program may use at most 128 MiB of HBM per device.

```python
import jax
import jax.numpy as jnp
from jax import lax

NCOL = 2048
COARSEN = 8
NROW = 512
NC = 32


def block_levels(key, extent, split, smallest, high):
    def one(axis_at, parts):
        heights = jax.random.uniform(jax.random.fold_in(jax.random.fold_in(key, 6), axis_at), (parts,), jnp.float32, smallest / len(split), high / len(split))
        return jnp.repeat(jnp.exp(heights), extent[axis_at] // parts).reshape((-1,) + (1,) * (len(extent) - axis_at - 1))

    gain = one(*split[0])
    for cut in split[1:]:
        gain = gain * one(*cut)
    return gain


def bell_draw(stream_key, shape, deviation, bound, split=(), held_as=jnp.bfloat16):
    values = deviation * jax.random.normal(stream_key, shape, jnp.float32)
    if split:
        values = values * block_levels(stream_key, shape, split, -0.22, 0.18)
    return jnp.clip(values, -bound, bound).astype(held_as)


def setup_inputs(seed: int = 0) -> dict:
    streams_of = jax.random.split(jax.random.key(seed), 7)
    return {
        "coarse_guess": bell_draw(streams_of[0], (NC, NROW, NCOL), 1.0, 2.5, ((0, 16), (1, 16)), jnp.float32),
        "initial": bell_draw(streams_of[1], (NROW, NCOL), 1.0, 2.5, ((0, 16),), jnp.float32),
        "diffusion": jnp.clip(0.002 + 0.006 * jax.random.uniform(streams_of[2], (NROW, NCOL), jnp.float32) ** block_levels(streams_of[2], (NROW, NCOL), ((0, 16),), -0.2, 0.2), 0.002, 0.008),
        "velocity": jnp.clip(jax.random.uniform(streams_of[3], (2, NROW, NCOL), jnp.float32, -0.04, 0.04) * block_levels(streams_of[3], (2, NROW, NCOL), ((1, 16),), -0.4, 0.0), -0.04, 0.04),
        "reaction": jnp.clip(0.002 + 0.003999999957159162 * jax.random.uniform(streams_of[4], (NROW, NCOL), jnp.float32) ** block_levels(streams_of[4], (NROW, NCOL), ((0, 16),), -0.2, 0.2), 0.002, 0.006),
        "source": bell_draw(streams_of[5], (NROW, NCOL), 0.05, 0.2, ((0, 16),), jnp.float32),
    }


def advance(padded, coefficients, factor):
    diffusion = coefficients[0]
    vel_row = coefficients[1]
    vel_col = coefficients[2]
    reaction = coefficients[3]
    source = coefficients[4]
    centre = padded[..., 1:-1, :]
    upper_row = padded[..., :-2, :]
    lower_row = padded[..., 2:, :]
    left_cell = jnp.roll(centre, 1, axis=-1)
    right_cell = jnp.roll(centre, -1, axis=-1)
    laplace = upper_row + lower_row + left_cell + right_cell - 4.0 * centre
    transport = jnp.maximum(vel_row, 0.0) * (centre - upper_row) + jnp.minimum(vel_row, 0.0) * (lower_row - centre)
    transport = transport + jnp.maximum(vel_col, 0.0) * (centre - left_cell) + jnp.minimum(vel_col, 0.0) * (right_cell - centre)
    change = diffusion * laplace + reaction * (centre - centre * centre * centre) + source - transport
    return centre + factor * change


def pad_rows(field):
    return jnp.pad(field, ((1, 1), (0, 0)))


def fine_prop(field, coefficients):
    for repeat in range(COARSEN):
        field = advance(pad_rows(field), coefficients, 1.0)
    return field


def coarse_prop(field, coefficients):
    return advance(pad_rows(field), coefficients, float(COARSEN))


def reference(coarse_guess, initial, diffusion, velocity, reaction, source):
    coefficients = jnp.stack([diffusion, velocity[0], velocity[1], reaction, source])
    starts = jnp.concatenate([initial[None], coarse_guess[:-1]], axis=0)
    relaxed = lax.map(lambda field: fine_prop(field, coefficients), starts)
    again = jnp.concatenate([initial[None], relaxed[:-1]], axis=0)
    forcing = lax.map(lambda field: fine_prop(field, coefficients) - coarse_prop(field, coefficients), again)

    def solve_turn(field, forcing_term):
        nxt_field = coarse_prop(field, coefficients) + forcing_term
        return nxt_field, nxt_field

    final_field, corrected = lax.scan(solve_turn, initial, forcing)
    return corrected
```

```python
import functools

import jax
import jax.numpy as jnp
from jax import lax
from jax.experimental import pallas as pl
from jax.experimental.pallas import tpu as pltpu
from jax.sharding import PartitionSpec as P

MESH = pl.DeviceIdType.MESH
F32 = jnp.float32

OFF = 16
ROWS = 64
MAIN = 32
HALO = 12
TILE = 128

Z0, Z1, R1 = 4, 5, 6
C0 = 7
NW = 9

NSEM = 64


def kernel(
    cg, init, dif, vel, rea, src,
    out,
    st, co, cc, w, fc, v, obuf,
    lsem, ssem, rsem, csend, crecv, xsend, xrecv,
):
    t = lax.axis_index("tm")
    s = lax.axis_index("space")
    z, core = t // 2, t % 2
    odd = s % 2 == 1
    has_up, has_dn = s > 0, s < 15

    lane = lax.broadcasted_iota(jnp.int32, (8, 128), 1)
    first_lane, last_lane = lane == 0, lane == 127

    loads = [
        (None, dif, st.at[0, pl.ds(2 * TILE, 512)]),
        (None, vel, st.at[pl.ds(1, 2), pl.ds(2 * TILE, 512)]),
        (None, rea, st.at[3, pl.ds(2 * TILE, 512)]),
        (None, src, st.at[4, pl.ds(2 * TILE, 512)]),
        (None, cg.at[0], st.at[6, pl.ds(2 * TILE, 512)]),
        (t == 0, init, st.at[5, pl.ds(2 * TILE, 512)]),
    ]

    def when(cond, body):
        if cond is None:
            body()
        else:
            pl.when(cond)(body)

    for i, (cond, a, b) in enumerate(loads):
        when(cond, lambda a=a, b=b, i=i: pltpu.make_async_copy(a, b, lsem.at[i]).start())

    partners = []
    for dt in (-2, -1, 0, 1, 2):
        for ds in (-1, 0, 1):
            if dt == 0 and ds == 0:
                continue
            ok = (t + dt >= 0) & (t + dt <= 15) & (s + ds >= 0) & (s + ds <= 15)
            partners.append((ok, t + dt, s + ds))
    barrier = pltpu.get_barrier_semaphore()
    count = 0
    for ok, pt, ps in partners:
        @pl.when(ok)
        def _(pt=pt, ps=ps):
            pl.semaphore_signal(barrier, inc=1, device_id=(pt, ps), device_id_type=MESH)
        count = count + ok.astype(jnp.int32)

    zero = jnp.zeros((8, 128), F32)

    def clear(at_stage, rows):
        def body(i, _):
            for q in range(7):
                st[q, pl.ds(at_stage + i * 8, 8), :] = zero
            return 0

        lax.fori_loop(0, 32, body, 0)

        def rows_body(i, _):
            for b in (Z0, Z1):
                for h in range(2):
                    w[b, OFF + rows + i, h] = zero
            for h in range(2):
                v[0, OFF + rows + i, h] = zero
            return 0

        lax.fori_loop(0, HALO, rows_body, 0)

    pl.when(s == 0)(lambda: clear(0, -HALO))
    pl.when(s == 15)(lambda: clear(6 * TILE, MAIN))

    pl.semaphore_wait(barrier, count)

    used = [0]

    def remote(source, dest, device, sends, receives):
        i = used[0]
        used[0] += 1
        cp = pltpu.make_async_remote_copy(
            src_ref=source, dst_ref=dest, send_sem=ssem.at[i], recv_sem=rsem.at[i],
            device_id=device, device_id_type=MESH,
        )
        return sends, receives, cp

    def start(copies):
        for sends, _, cp in copies:
            pl.when(sends)(lambda cp=cp: cp.start())

    def wait_recv(copies):
        for _, receives, cp in copies:
            pl.when(receives)(lambda cp=cp: cp.wait_recv())

    def wait_send(copies):
        for sends, _, cp in copies:
            pl.when(sends)(lambda cp=cp: cp.wait_send())

    later_t, had_t = t < 15, t > 0
    yes = t >= 0
    near, far = [], []
    for group, up_from, up_to, dn_from, dn_to in (
        (near, 3 * TILE, 1 * TILE, 0, 6 * TILE),
        (far, 2 * TILE, 0, TILE, 7 * TILE),
    ):
        for a, b in ((dif, 0), (vel, None), (rea, 3), (src, 4)):
            def part(at, a=a):
                return a.at[:, pl.ds(at, TILE)] if len(a.shape) == 3 else a.at[pl.ds(at, TILE)]

            def stage(at, b=b):
                return st.at[pl.ds(1, 2), pl.ds(at, TILE)] if b is None else st.at[b, pl.ds(at, TILE)]

            group.append(remote(part(up_from), stage(up_to), (t, s + 1), has_dn, has_up))
            group.append(remote(part(dn_from), stage(dn_to), (t, s - 1), has_up, has_dn))
    own = [
        remote(cg.at[0, pl.ds(3 * TILE, TILE)], st.at[6, pl.ds(TILE, TILE)], (t, s + 1), has_dn, has_up),
        remote(cg.at[0, pl.ds(0, TILE)], st.at[6, pl.ds(6 * TILE, TILE)], (t, s - 1), has_up, has_dn),
    ]
    nxt = [
        remote(cg.at[1], st.at[5, pl.ds(2 * TILE, 512)], (t + 1, s), later_t, had_t),
        remote(cg.at[1, pl.ds(3 * TILE, TILE)], st.at[5, pl.ds(TILE, TILE)], (t + 1, s + 1), later_t & has_dn, had_t & has_up),
        remote(cg.at[1, pl.ds(0, TILE)], st.at[5, pl.ds(6 * TILE, TILE)], (t + 1, s - 1), later_t & has_up, had_t & has_dn),
    ]
    ini = [
        remote(init.at[pl.ds(3 * TILE, TILE)], st.at[5, pl.ds(TILE, TILE)], (t, s + 1), (t == 0) & has_dn, (t == 0) & has_up),
        remote(init.at[pl.ds(0, TILE)], st.at[5, pl.ds(6 * TILE, TILE)], (t, s - 1), (t == 0) & has_up, (t == 0) & has_dn),
    ]
    first = near + own + ini + nxt
    start(first)
    start(far)

    def staged(q, tile, r8, h):
        return st[q, pl.ds(tile * TILE + r8 + 8 * h, 8, stride=16), :]

    def coefficients(tile_lo, tiles):
        def body(i, _):
            tile = tile_lo + i
            for r8 in range(8):
                row = tile * 8 + r8
                for h in range(2):
                    d, b, c, k, sr = [staged(q, tile, r8, h) for q in range(5)]
                    u = d + jnp.maximum(b, 0.0)
                    n = d - jnp.minimum(b, 0.0)
                    le = d + jnp.maximum(c, 0.0)
                    ri = d - jnp.minimum(c, 0.0)
                    a = k - ((u + n) + (le + ri))
                    co[0, row, h] = 1.0 + a
                    co[1, row, h] = k
                    co[2, row, h] = u
                    co[3, row, h] = n
                    co[4, row, h] = le
                    co[5, row, h] = ri
                    co[6, row, h] = sr
            return 0

        lax.fori_loop(0, tiles, body, 0)

    def coarse_coefficients():
        def body(i, _):
            for j in range(4):
                row = OFF - 4 + i * 4 + j
                for h in range(2):
                    k, u, n, le, ri, sr = [8.0 * co[q, row, h] for q in range(1, 7)]
                    cc[0, row, h] = 1.0 + (k - ((u + n) + (le + ri)))
                    for q, x in enumerate((k, u, n, le, ri, sr)):
                        cc[1 + q, row, h] = x
            return 0

        lax.fori_loop(0, 10, body, 0)

    def field(q, dest, tile_lo, tiles):
        def body(i, _):
            tile = tile_lo + i
            for r8 in range(8):
                for h in range(2):
                    w[dest, tile * 8 + r8, h] = staged(q, tile, r8, h)
            return 0

        lax.fori_loop(0, tiles, body, 0)

    def sides(a, b):
        ra, rb = pltpu.roll(a, 1, 1), pltpu.roll(b, 1, 1)
        la = jnp.where(first_lane, pltpu.roll(rb, 1, 0), ra)
        lb = jnp.where(first_lane, ra, rb)
        qa, qb = pltpu.roll(a, 127, 1), pltpu.roll(b, 127, 1)
        ga = jnp.where(last_lane, qb, qa)
        gb = jnp.where(last_lane, pltpu.roll(qa, 7, 0), qb)
        return (la, lb), (ga, gb)

    def step(state, coef, base, n, emit):
        load = lambda row: [state[row, h] for h in range(2)]
        up, ce = load(base - 1), load(base)
        for r in range(n):
            row = base + r
            dn = load(row + 1)
            left, right = sides(*ce)
            for h in range(2):
                a, k, u, d, le, ri, sr = [coef[q, row, h] for q in range(7)]
                x = ce[h]
                y = x * (a - k * (x * x)) + sr
                y = y + u * up[h] + d * dn[h]
                y = y + le * left[h] + ri * right[h]
                emit(r, row, h, y, x)
            up, ce = ce, dn

    for i, (cond, a, b) in enumerate(loads):
        when(cond, lambda a=a, b=b, i=i: pltpu.make_async_copy(a, b, lsem.at[i]).wait())
    coefficients(2, 4)
    field(6, 2, 2, 4)
    wait_recv(near + own + ini + nxt)
    coefficients(1, 1)
    coefficients(6, 1)
    field(6, 2, 1, 1)
    field(6, 2, 6, 1)
    field(5, 0, 1, 6)

    edge_r0 = [
        remote(w.at[Z1, pl.ds(OFF + MAIN - HALO, HALO)], w.at[Z1, pl.ds(OFF - HALO, HALO)], (t, s + 1), has_dn, has_up),
        remote(w.at[Z1, pl.ds(OFF, HALO)], w.at[Z1, pl.ds(OFF + MAIN, HALO)], (t, s - 1), has_up, has_dn),
    ]
    move_r1 = [
        remote(w.at[R1, pl.ds(OFF, MAIN)], w.at[Z0, pl.ds(OFF, MAIN)], (t + 1, s), later_t, had_t),
        remote(w.at[R1, pl.ds(OFF + MAIN - HALO, HALO)], w.at[Z0, pl.ds(OFF - HALO, HALO)], (t + 1, s + 1), later_t & has_dn, had_t & has_up),
        remote(w.at[R1, pl.ds(OFF, HALO)], w.at[Z0, pl.ds(OFF + MAIN, HALO)], (t + 1, s - 1), later_t & has_up, had_t & has_dn),
    ]

    def relax(i, _):
        f = 1 - i

        def one(k, _):
            a = 2 * f + k % 2
            b = 2 * f + 1 - k % 2

            def emit(r, row, h, y, x):
                w[b, row, h] = y

            step(w.at[a], co, OFF - 7, 46, emit)
            return 0

        lax.fori_loop(0, 7, one, 0)
        dest = Z1 + f

        def emit(r, row, h, y, x):
            w[dest, row, h] = y

        step(w.at[2 * f + 1], co, OFF, MAIN, emit)
        pl.when(f == 1)(lambda: start(move_r1))
        return 0

    lax.fori_loop(0, 2, relax, 0)
    start(edge_r0)
    wait_recv(far)
    coefficients(0, 1)
    coefficients(7, 1)
    coarse_coefficients()

    def again(i, _):
        f = 1 - i
        pl.when(f == 1)(lambda: wait_recv(edge_r0))
        pl.when(f == 0)(lambda: wait_recv(move_r1))

        def emit_first(r, row, h, y, x):
            w[2 * f, row, h] = y
            if 7 <= r < 47:
                w[C0 + f, row, h] = 8.0 * y - 7.0 * x

        step(w.at[Z0 + f], co, OFF - 11, 54, emit_first)

        def one(k, _):
            a = 2 * f + k % 2
            b = 2 * f + 1 - k % 2

            def emit(r, row, h, y, x):
                w[b, row, h] = y

            step(w.at[a], co, OFF - 10, 52, emit)
            return 0

        lax.fori_loop(0, 6, one, 0)

        def emit_last(r, row, h, y, x):
            w[2 * f + 1, row, h] = y
            fc[2 * core + f, row, h] = y - w[C0 + f, row, h]

        step(w.at[2 * f], co, OFF - 4, 40, emit_last)
        return 0

    lax.fori_loop(0, jnp.where(t == 0, 1, 2), again, 0)

    give_f = [
        remote(fc.at[pl.ds(2, 2), pl.ds(OFF - 4, 40)], fc.at[pl.ds(2, 2), pl.ds(OFF - 4, 40)], (t - 1, s), core == 1, core == 0),
    ]
    start(give_f)

    def chunk_row(m):
        return OFF + jnp.where(odd, 4 * m, 28 - 4 * m)

    def main_copy(m):
        rows = pl.ds(chunk_row(m), 4)
        return pltpu.make_async_remote_copy(
            src_ref=v.at[4, rows], dst_ref=v.at[0, rows], send_sem=csend.at[m], recv_sem=crecv.at[m],
            device_id=(t + 2, s), device_id_type=MESH,
        )

    def edge_copy(i, from_row, to_row, ds):
        return pltpu.make_async_remote_copy(
            src_ref=v.at[4, pl.ds(from_row, 4)], dst_ref=v.at[0, pl.ds(to_row, 4)],
            send_sem=csend.at[8 + i], recv_sem=crecv.at[8 + i],
            device_id=(t + 2, s + ds), device_id_type=MESH,
        )

    low_from, low_to = OFF, OFF + MAIN
    top_from, top_to = OFF + MAIN - 4, OFF - 4

    def give_copy(m):
        rows = pl.ds(chunk_row(m), 4)
        return pltpu.make_async_remote_copy(
            src_ref=v.at[pl.ds(3, 2), rows], dst_ref=v.at[pl.ds(3, 2), rows],
            send_sem=xsend.at[m], recv_sem=xrecv.at[m], device_id=(t + 1, s), device_id_type=MESH,
        )

    def to_out(state, o, row):
        tile = (row - OFF) // 8
        r8 = (row - OFF) % 8
        for h in range(2):
            obuf[o, pl.ds(tile * TILE + r8 + 8 * h, 8, stride=16), :] = state[row, h]

    def send_edges(m):
        pl.when((m == 0) & odd)(lambda: edge_copy(0, low_from, low_to, -1).start())
        pl.when((m == 0) & jnp.logical_not(odd))(lambda: edge_copy(0, top_from, top_to, 1).start())
        pl.when((m == 7) & odd & has_dn)(lambda: edge_copy(1, top_from, top_to, 1).start())
        pl.when((m == 7) & jnp.logical_not(odd) & has_up)(lambda: edge_copy(1, low_from, low_to, -1).start())

    end_edge = jnp.where(odd, has_dn, has_up)

    def chain():
        wait_recv(give_f)
        pl.when(z == 0)(lambda: copy_rows(3, v, 2, OFF - 4, 40))

        def level(k, base, n):
            def emit(r, row, h, y, x):
                v[k, row, h] = y + fc[k - 1, row, h]

            step(v.at[k - 1], cc, base, n, emit)

        def base_of(i, k):
            return OFF + jnp.where(odd, 4 * i - 4 - k, 32 - 4 * i + k)

        def turn(i, _):
            @pl.when(z > 0)
            def _():
                @pl.when(i == 1)
                def _():
                    edge_copy(0, low_from, low_to, 0).wait_recv()

                pl.when(i < 9)(lambda: main_copy(jnp.minimum(i - 1, 7)).wait_recv())
                pl.when((i == 9) & end_edge)(lambda: edge_copy(1, low_from, low_to, 0).wait_recv())
                pl.when(i == 1)(lambda: level(1, base_of(0, 1), 4))
                level(1, base_of(i, 1), 4)
                level(2, base_of(i, 2), 4)

            level(3, base_of(i, 3), 4)

            @pl.when(i > 1)
            def _():
                level(4, base_of(i, 4), 4)
                m = i - 2

                @pl.when(z < 7)
                def _():
                    main_copy(m).start()
                    send_edges(m)

                give_copy(m).start()

            return 0

        lax.fori_loop(1, 10, turn, 0)

    def copy_rows(source, to, dest, base, n):
        def body(i, _):
            for j in range(4):
                for h in range(2):
                    to[dest, base + 4 * i + j, h] = w[source, base + 4 * i + j, h]
            return 0

        lax.fori_loop(0, n // 4, body, 0)

    def finish_first():
        pl.when(z == 0)(lambda: copy_rows(Z1, v, 1, OFF, MAIN))

        def body(i, _):
            for j in range(4):
                to_out(v.at[1], 0, OFF + 4 * i + j)
                to_out(v.at[2], 1, OFF + 4 * i + j)
            return 0

        lax.fori_loop(0, 8, body, 0)

    def finish_second():
        def body(m, _):
            give_copy(m).wait_recv()
            for j in range(4):
                to_out(v.at[3], 0, chunk_row(m) + j)
                to_out(v.at[4], 1, chunk_row(m) + j)
            return 0

        lax.fori_loop(0, 8, body, 0)

    @pl.when(core == 0)
    def _():
        chain()
        finish_first()

    pl.when(core == 1)(finish_second)
    done = pltpu.make_async_copy(obuf, out, lsem.at[0])
    done.start()

    wait_send(near + far + own + ini + nxt + edge_r0 + move_r1 + give_f)

    @pl.when(core == 0)
    def _():
        def drain(m, _):
            pl.when(z < 7)(lambda: main_copy(m).wait_send())
            give_copy(m).wait_send()
            return 0

        lax.fori_loop(0, 8, drain, 0)
        pl.when(z < 7)(lambda: edge_copy(0, low_from, low_to, 0).wait_send())
        pl.when((z < 7) & end_edge)(lambda: edge_copy(1, low_from, low_to, 0).wait_send())

    done.wait()


def tiles(x):
    lead = x.shape[:-2]
    n = len(lead)
    y = x.reshape(lead + (4, 8, 16, 128))
    y = y.transpose(tuple(range(n)) + (n, n + 2, n + 1, n + 3))
    return y.reshape(lead + (512, 128))


def shards(coarse_guess, initial, diffusion, velocity, reaction, source):
    hbm = pl.BlockSpec(memory_space=pl.ANY)
    state = (2, 8, 128)
    out = pl.pallas_call(
        kernel,
        out_shape=jax.ShapeDtypeStruct((2, 512, 128), F32),
        in_specs=[hbm] * 6,
        out_specs=hbm,
        scratch_shapes=[
            pltpu.VMEM((7, 8 * TILE, 128), F32),
            pltpu.VMEM((7, ROWS) + state, F32),
            pltpu.VMEM((7, ROWS) + state, F32),
            pltpu.VMEM((NW, ROWS) + state, F32),
            pltpu.VMEM((4, ROWS) + state, F32),
            pltpu.VMEM((5, ROWS) + state, F32),
            pltpu.VMEM((2, 512, 128), F32),
            pltpu.SemaphoreType.DMA((8,)),
            pltpu.SemaphoreType.DMA((NSEM,)),
            pltpu.SemaphoreType.DMA((NSEM,)),
            pltpu.SemaphoreType.DMA((10,)),
            pltpu.SemaphoreType.DMA((10,)),
            pltpu.SemaphoreType.DMA((8,)),
            pltpu.SemaphoreType.DMA((8,)),
        ],
        compiler_params=pltpu.CompilerParams(
            collective_id=0, has_side_effects=True, vmem_limit_bytes=48 * 2**20
        ),
    )(tiles(coarse_guess), tiles(initial), tiles(diffusion), tiles(velocity), tiles(reaction), tiles(source))
    out = out.reshape(2, 4, 16, 8, 128).transpose(0, 1, 3, 2, 4)
    return out.reshape(2, 32, 2048)


def solution(mesh):
    return jax.shard_map(
        shards,
        mesh=mesh,
        in_specs=(
            P("tm", "space", None),
            P("space", None),
            P("space", None),
            P(None, "space", None),
            P("space", None),
            P("space", None),
        ),
        out_specs=P("tm", "space", None),
        check_vma=False,
    )
```

```python
import functools

import jax
import jax.numpy as jnp
from jax import lax
from jax.experimental import pallas as pl
from jax.experimental.pallas import tpu as pltpu
from jax.sharding import PartitionSpec as P

MESH = pl.DeviceIdType.MESH
F32 = jnp.float32

OFF = 16
ROWS = 64
MAIN = 32
HALO = 12
TILE = 128


NSEM = 64


def kernel(
    cg, init, dif, vel, rea, src,
    out,
    st, co, cc, ping, pong, again_in, first_coarse, fc, v, prev, obuf,
    lsem, ssem, rsem, esend, erecv, csend, crecv, xsend, xrecv, fsend, frecv,
):
    t = lax.axis_index("tm")
    s = lax.axis_index("space")
    t_last, s_last = lax.axis_size("tm") - 1, lax.axis_size("space") - 1
    z_last = t_last // 2
    z, core = t // 2, t % 2
    odd = s % 2 == 1
    has_up, has_dn = s > 0, s < s_last
    origin = t == t_last

    lane = lax.broadcasted_iota(jnp.int32, (8, 128), 1)
    first_lane, last_lane = lane == 0, lane == 127

    loads = [
        (None, dif, st.at[0, pl.ds(2 * TILE, 512)]),
        (None, vel, st.at[pl.ds(1, 2), pl.ds(2 * TILE, 512)]),
        (None, rea, st.at[3, pl.ds(2 * TILE, 512)]),
        (None, src, st.at[4, pl.ds(2 * TILE, 512)]),
        (t < t_last, cg.at[0], st.at[5, pl.ds(2 * TILE, 512)]),
        (t < t_last, cg.at[1], st.at[6, pl.ds(2 * TILE, 512)]),
        (origin, init, st.at[5, pl.ds(2 * TILE, 512)]),
    ]

    def when(cond, body):
        if cond is None:
            body()
        else:
            pl.when(cond)(body)

    for i, (cond, a, b) in enumerate(loads):
        when(cond, lambda a=a, b=b, i=i: pltpu.make_async_copy(a, b, lsem.at[i]).start())

    partners = []

    def partner(ok, pt, ps):
        partners.append((ok & (ps >= 0) & (ps <= s_last), pt, ps))

    for ds in (-1, 1):
        partner(t >= 0, t, s + ds)
    for ds in (-1, 0, 1):
        partner((core == 0) & (z > 0), t - 2, s + ds)
        partner((core == 0) & (z < z_last), t + 2, s + ds)
    partner(t > 0, t - 1, s)
    partner(t < t_last, t + 1, s)
    partner((t == 0) | origin, t_last - t, s)
    barrier = pltpu.get_barrier_semaphore()
    count = 0
    for ok, pt, ps in partners:
        @pl.when(ok)
        def _(pt=pt, ps=ps):
            pl.semaphore_signal(barrier, inc=1, device_id=(pt, ps), device_id_type=MESH)
        count = count + ok.astype(jnp.int32)

    zero = jnp.zeros((8, 128), F32)

    def clear(at_stage, rows):
        def body(i, _):
            for q in range(7):
                st[q, pl.ds(at_stage + i * 8, 8), :] = zero
            return 0

        lax.fori_loop(0, 32, body, 0)

        def rows_body(i, _):
            for b in range(2):
                for h in range(2):
                    again_in[b, OFF + rows + i, h] = zero
            for h in range(2):
                v[0, OFF + rows + i, h] = zero
            return 0

        lax.fori_loop(0, HALO, rows_body, 0)

    pl.when(s == 0)(lambda: clear(0, -HALO))
    pl.when(s == s_last)(lambda: clear(6 * TILE, MAIN))

    pl.semaphore_wait(barrier, count)

    used = [0]

    def remote(source, dest, device, sends, receives):
        i = used[0]
        used[0] += 1
        cp = pltpu.make_async_remote_copy(
            src_ref=source, dst_ref=dest, send_sem=ssem.at[i], recv_sem=rsem.at[i],
            device_id=device, device_id_type=MESH,
        )
        return sends, receives, cp

    def start(copies):
        for sends, _, cp in copies:
            pl.when(sends)(lambda cp=cp: cp.start())

    def wait_recv(copies):
        for _, receives, cp in copies:
            pl.when(receives)(lambda cp=cp: cp.wait_recv())

    def wait_send(copies):
        for sends, _, cp in copies:
            pl.when(sends)(lambda cp=cp: cp.wait_send())

    near, far, near_on, far_on = [], [], [], []
    half = pl.multiple_of(core * (TILE // 2), TILE // 2)
    sibling = (t + 1 - 2 * core, s)
    for group, onward, up_from, up_to, dn_from, dn_to in (
        (near, near_on, 3 * TILE, 1 * TILE, 0, 6 * TILE),
        (far, far_on, 2 * TILE, 0, TILE, 7 * TILE),
    ):
        for a, b in ((dif, 0), (vel, None), (rea, 3), (src, 4)):
            def part(at, a=a):
                rows = pl.ds(at + half, TILE // 2)
                return a.at[:, rows] if len(a.shape) == 3 else a.at[rows]

            def stage(at, b=b):
                rows = pl.ds(at + half, TILE // 2)
                return st.at[pl.ds(1, 2), rows] if b is None else st.at[b, rows]

            group.append(remote(part(up_from), stage(up_to), (t, s + 1), has_dn, has_up))
            group.append(remote(part(dn_from), stage(dn_to), (t, s - 1), has_up, has_dn))
            onward.append(remote(stage(up_to), stage(up_to), sibling, has_up, has_up))
            onward.append(remote(stage(dn_to), stage(dn_to), sibling, has_dn, has_dn))
    fields = []
    for a, b, mine in ((cg.at[0], 5, t < t_last), (cg.at[1], 6, t < t_last), (init, 5, origin)):
        fields += [
            remote(a.at[pl.ds(3 * TILE, TILE)], st.at[b, pl.ds(TILE, TILE)], (t, s + 1), mine & has_dn, mine & has_up),
            remote(a.at[pl.ds(0, TILE)], st.at[b, pl.ds(6 * TILE, TILE)], (t, s - 1), mine & has_up, mine & has_dn),
        ]
    start(near)
    start(fields)
    start(far)

    def staged(q, tile, r8, h):
        return st[q, pl.ds(tile * TILE + r8 + 8 * h, 8, stride=16), :]

    def coefficients(tile_lo, tiles):
        def body(i, _):
            tile = tile_lo + i
            for r8 in range(8):
                row = tile * 8 + r8
                for h in range(2):
                    d, b, c, k, sr = [staged(q, tile, r8, h) for q in range(5)]
                    u = d + jnp.maximum(b, 0.0)
                    n = d - jnp.minimum(b, 0.0)
                    le = d + jnp.maximum(c, 0.0)
                    ri = d - jnp.minimum(c, 0.0)
                    a = k - ((u + n) + (le + ri))
                    co[0, row, h] = 1.0 + a
                    co[1, row, h] = k
                    co[2, row, h] = u
                    co[3, row, h] = n
                    co[4, row, h] = le
                    co[5, row, h] = ri
                    co[6, row, h] = sr
            return 0

        lax.fori_loop(0, tiles, body, 0)

    def coarse_coefficients():
        def body(i, _):
            for j in range(4):
                row = OFF - 4 + i * 4 + j
                for h in range(2):
                    k, u, n, le, ri, sr = [8.0 * co[q, row, h] for q in range(1, 7)]
                    cc[0, row, h] = 1.0 + (k - ((u + n) + (le + ri)))
                    for q, x in enumerate((k, u, n, le, ri, sr)):
                        cc[1 + q, row, h] = x
            return 0

        lax.fori_loop(0, 10, body, 0)

    def field(q, dest, tile_lo, tiles):
        def body(i, _):
            tile = tile_lo + i
            for r8 in range(8):
                for h in range(2):
                    ping[dest, tile * 8 + r8, h] = staged(q, tile, r8, h)
            return 0

        lax.fori_loop(0, tiles, body, 0)

    def sides(a, b):
        ra, rb = pltpu.roll(a, 1, 1), pltpu.roll(b, 1, 1)
        la = jnp.where(first_lane, pltpu.roll(rb, 1, 0), ra)
        lb = jnp.where(first_lane, ra, rb)
        qa, qb = pltpu.roll(a, 127, 1), pltpu.roll(b, 127, 1)
        ga = jnp.where(last_lane, qb, qa)
        gb = jnp.where(last_lane, pltpu.roll(qa, 7, 0), qb)
        return (la, lb), (ga, gb)

    def step(state, coef, base, n, emit):
        load = lambda row: [state[row, h] for h in range(2)]
        up, ce = load(base - 1), load(base)
        for r in range(n):
            row = base + r
            dn = load(row + 1)
            left, right = sides(*ce)
            for h in range(2):
                a, k, u, d, le, ri, sr = [coef[q, row, h] for q in range(7)]
                x = ce[h]
                y = x * (a - k * (x * x)) + sr
                y = y + u * up[h] + d * dn[h]
                y = y + le * left[h] + ri * right[h]
                emit(r, row, h, y, x)
            up, ce = ce, dn

    for i, (cond, a, b) in enumerate(loads):
        when(cond, lambda a=a, b=b, i=i: pltpu.make_async_copy(a, b, lsem.at[i]).wait())
    coefficients(2, 4)
    field(5, 0, 2, 4)
    field(6, 1, 2, 4)
    wait_recv(near)
    start(near_on)
    wait_recv(fields)
    for q in range(2):
        field(5 + q, q, 1, 1)
        field(5 + q, q, 6, 1)
    wait_recv(near_on)
    coefficients(1, 1)
    coefficients(6, 1)

    def edge(f, side):
        from_row, to_row = ((OFF + MAIN - HALO, OFF - HALO), (OFF, OFF + MAIN))[side]
        return pltpu.make_async_remote_copy(
            src_ref=again_in.at[f, pl.ds(from_row, HALO)], dst_ref=again_in.at[f, pl.ds(to_row, HALO)],
            send_sem=esend.at[2 * f + side], recv_sem=erecv.at[2 * f + side],
            device_id=(t, s + 1 - 2 * side), device_id_type=MESH,
        )

    n_fields = jnp.where(origin, 1, 2)

    def keep(dest, f):
        def emit(r, row, h, y, x):
            dest[f, row, h] = y

        return emit

    def relax(f, _):
        def two(k, _):
            step(ping.at[f], co, OFF - 7, 46, keep(pong, f))
            step(pong.at[f], co, OFF - 6, 44, keep(ping, f))
            return 0

        lax.fori_loop(0, 3, two, 0)
        step(ping.at[f], co, OFF - 1, 34, keep(pong, f))
        step(pong.at[f], co, OFF, MAIN, keep(again_in, f))
        pl.when(has_dn)(lambda: edge(f, 0).start())
        pl.when(has_up)(lambda: edge(f, 1).start())
        return 0

    lax.fori_loop(0, n_fields, relax, 0)

    def first_copy(m):
        rows = pl.ds(chunk_row(m), 4)
        return pltpu.make_async_remote_copy(
            src_ref=again_in.at[0, rows], dst_ref=prev.at[rows], send_sem=fsend.at[m], recv_sem=frecv.at[m],
            device_id=(0, s), device_id_type=MESH,
        )

    def chunk_row(m):
        return OFF + jnp.where(odd, 4 * m, 28 - 4 * m)

    def each_chunk(body):
        def one(m, _):
            body(m)
            return 0

        lax.fori_loop(0, 8, one, 0)

    pl.when(origin)(lambda: each_chunk(lambda m: first_copy(m).start()))
    wait_recv(far)
    start(far_on)
    wait_recv(far_on)
    coefficients(0, 1)
    coefficients(7, 1)
    coarse_coefficients()

    def again(f, _):
        pl.when(has_up)(lambda: edge(f, 0).wait_recv())
        pl.when(has_dn)(lambda: edge(f, 1).wait_recv())

        def emit_first(r, row, h, y, x):
            ping[f, row, h] = y
            if 7 <= r < 47:
                first_coarse[f, row, h] = 8.0 * y - 7.0 * x

        step(again_in.at[f], co, OFF - 11, 54, emit_first)

        def two(k, _):
            step(ping.at[f], co, OFF - 10, 52, keep(pong, f))
            step(pong.at[f], co, OFF - 9, 50, keep(ping, f))
            return 0

        lax.fori_loop(0, 3, two, 0)

        def emit_last(r, row, h, y, x):
            pong[f, row, h] = y
            fc[2 * core + f, row, h] = y - first_coarse[f, row, h]

        step(ping.at[f], co, OFF - 4, 40, emit_last)
        return 0

    lax.fori_loop(0, n_fields, again, 0)

    give_f = [
        remote(fc.at[pl.ds(2, 2), pl.ds(OFF - 4, 40)], fc.at[pl.ds(2, 2), pl.ds(OFF - 4, 40)], (t - 1, s), (core == 1) & (z < z_last), (core == 0) & (z < z_last)),
    ]
    start(give_f)

    def main_copy(m):
        rows = pl.ds(chunk_row(m), 4)
        return pltpu.make_async_remote_copy(
            src_ref=v.at[4, rows], dst_ref=v.at[0, rows], send_sem=csend.at[m], recv_sem=crecv.at[m],
            device_id=(t + 2, s), device_id_type=MESH,
        )

    def edge_copy(i, from_row, to_row, ds):
        return pltpu.make_async_remote_copy(
            src_ref=v.at[4, pl.ds(from_row, 4)], dst_ref=v.at[0, pl.ds(to_row, 4)],
            send_sem=csend.at[8 + i], recv_sem=crecv.at[8 + i],
            device_id=(t + 2, s + ds), device_id_type=MESH,
        )

    low_from, low_to = OFF, OFF + MAIN
    top_from, top_to = OFF + MAIN - 4, OFF - 4

    def origin_copy(at, i):
        rows = pl.ds(at, 4)
        return pltpu.make_async_remote_copy(
            src_ref=pong.at[0, rows], dst_ref=v.at[0, rows], send_sem=csend.at[i], recv_sem=crecv.at[i],
            device_id=(0, s), device_id_type=MESH,
        )

    end_edge = jnp.where(odd, has_dn, has_up)
    start_edge = OFF + jnp.where(odd, -4, MAIN)
    end_edge_row = OFF + jnp.where(odd, MAIN, -4)

    @pl.when(origin)
    def _():
        origin_copy(start_edge, 8).start()
        each_chunk(lambda m: origin_copy(chunk_row(m), m).start())
        pl.when(end_edge)(lambda: origin_copy(end_edge_row, 9).start())

    def give_copy(m):
        rows = pl.ds(chunk_row(m), 4)
        return pltpu.make_async_remote_copy(
            src_ref=v.at[pl.ds(1, 3), rows], dst_ref=v.at[pl.ds(1, 3), rows],
            send_sem=xsend.at[m], recv_sem=xrecv.at[m], device_id=(t + 1, s), device_id_type=MESH,
        )

    def onward_copy(m):
        rows = pl.ds(chunk_row(m), 4)
        return pltpu.make_async_remote_copy(
            src_ref=v.at[3, rows], dst_ref=prev.at[rows], send_sem=fsend.at[m], recv_sem=frecv.at[m],
            device_id=(t + 1, s), device_id_type=MESH,
        )

    def to_out(state, o, row):
        tile = (row - OFF) // 8
        r8 = (row - OFF) % 8
        for h in range(2):
            obuf[o, pl.ds(tile * TILE + r8 + 8 * h, 8, stride=16), :] = state[row, h]

    def send_edges(m):
        pl.when((m == 0) & odd)(lambda: edge_copy(0, low_from, low_to, -1).start())
        pl.when((m == 0) & jnp.logical_not(odd))(lambda: edge_copy(0, top_from, top_to, 1).start())
        pl.when((m == 7) & odd & has_dn)(lambda: edge_copy(1, top_from, top_to, 1).start())
        pl.when((m == 7) & jnp.logical_not(odd) & has_up)(lambda: edge_copy(1, low_from, low_to, -1).start())

    def chain():
        wait_recv(give_f)

        def level(k, base, n):
            def emit(r, row, h, y, x):
                v[k, row, h] = y + fc[k - 1, row, h]

            step(v.at[k - 1], cc, base, n, emit)

        def base_of(i, k):
            return OFF + jnp.where(odd, 4 * i - 4 - k, 32 - 4 * i + k)

        def turn(i, _):
            pl.when(i == 1)(lambda: edge_copy(0, low_from, low_to, 0).wait_recv())
            pl.when(i < 9)(lambda: main_copy(jnp.minimum(i - 1, 7)).wait_recv())
            pl.when((i == 9) & end_edge)(lambda: edge_copy(1, low_from, low_to, 0).wait_recv())
            pl.when(i == 1)(lambda: level(1, base_of(0, 1), 4))
            level(1, base_of(i, 1), 4)
            level(2, base_of(i, 2), 4)
            m = i - 2

            @pl.when(z < z_last)
            def _():
                level(3, base_of(i, 3), 4)

                @pl.when(i > 1)
                def _():
                    level(4, base_of(i, 4), 4)
                    send_edges(m)
                    main_copy(m).start()

            pl.when(i > 1)(lambda: give_copy(m).start())
            return 0

        lax.fori_loop(1, 10, turn, 0)

    def finish_first():
        def body(m):
            onward_copy(m).wait_recv()
            for j in range(4):
                to_out(prev, 0, chunk_row(m) + j)
                to_out(v.at[0], 1, chunk_row(m) + j)

        each_chunk(body)

    def finish_second():
        def body(m):
            give_copy(m).wait_recv()
            pl.when(z < z_last)(lambda: onward_copy(m).start())
            for j in range(4):
                to_out(v.at[1], 0, chunk_row(m) + j)
                to_out(v.at[2], 1, chunk_row(m) + j)

        each_chunk(body)

    @pl.when(core == 0)
    def _():
        chain()
        finish_first()

    pl.when(core == 1)(finish_second)
    done = pltpu.make_async_copy(obuf, out, lsem.at[0])
    done.start()

    wait_send(near + far + near_on + far_on + fields + give_f)

    def edges_left(f, _):
        pl.when(has_dn)(lambda: edge(f, 0).wait_send())
        pl.when(has_up)(lambda: edge(f, 1).wait_send())
        return 0

    lax.fori_loop(0, n_fields, edges_left, 0)

    @pl.when(core == 0)
    def _():
        def drain(m):
            pl.when(z < z_last)(lambda: main_copy(m).wait_send())
            give_copy(m).wait_send()

        each_chunk(drain)
        pl.when(z < z_last)(lambda: edge_copy(0, low_from, low_to, 0).wait_send())
        pl.when((z < z_last) & end_edge)(lambda: edge_copy(1, low_from, low_to, 0).wait_send())

    pl.when((core == 1) & (z < z_last))(lambda: each_chunk(lambda m: onward_copy(m).wait_send()))

    @pl.when(origin)
    def _():
        def drain(m):
            first_copy(m).wait_send()
            origin_copy(chunk_row(m), m).wait_send()

        each_chunk(drain)
        origin_copy(start_edge, 8).wait_send()
        pl.when(end_edge)(lambda: origin_copy(end_edge_row, 9).wait_send())

    done.wait()


def tiles(x):
    lead = x.shape[:-2]
    n = len(lead)
    y = x.reshape(lead + (4, 8, 16, 128))
    y = y.transpose(tuple(range(n)) + (n, n + 2, n + 1, n + 3))
    return y.reshape(lead + (512, 128))


def shards(coarse_guess, initial, diffusion, velocity, reaction, source):
    hbm = pl.BlockSpec(memory_space=pl.ANY)
    state = (2, 8, 128)
    out = pl.pallas_call(
        kernel,
        out_shape=jax.ShapeDtypeStruct((2, 512, 128), F32),
        in_specs=[hbm] * 6,
        out_specs=hbm,
        scratch_shapes=[
            pltpu.VMEM((7, 8 * TILE, 128), F32),
            pltpu.VMEM((7, ROWS) + state, F32),
            pltpu.VMEM((7, ROWS) + state, F32),
            pltpu.VMEM((2, ROWS) + state, F32),
            pltpu.VMEM((2, ROWS) + state, F32),
            pltpu.VMEM((2, ROWS) + state, F32),
            pltpu.VMEM((2, ROWS) + state, F32),
            pltpu.VMEM((4, ROWS) + state, F32),
            pltpu.VMEM((5, ROWS) + state, F32),
            pltpu.VMEM((ROWS,) + state, F32),
            pltpu.VMEM((2, 512, 128), F32),
            pltpu.SemaphoreType.DMA((8,)),
            pltpu.SemaphoreType.DMA((NSEM,)),
            pltpu.SemaphoreType.DMA((NSEM,)),
            pltpu.SemaphoreType.DMA((4,)),
            pltpu.SemaphoreType.DMA((4,)),
            pltpu.SemaphoreType.DMA((10,)),
            pltpu.SemaphoreType.DMA((10,)),
            pltpu.SemaphoreType.DMA((8,)),
            pltpu.SemaphoreType.DMA((8,)),
            pltpu.SemaphoreType.DMA((8,)),
            pltpu.SemaphoreType.DMA((8,)),
        ],
        compiler_params=pltpu.CompilerParams(
            collective_id=0, has_side_effects=True, vmem_limit_bytes=63 * 2**20
        ),
    )(tiles(coarse_guess), tiles(initial), tiles(diffusion), tiles(velocity), tiles(reaction), tiles(source))
    out = out.reshape(2, 4, 16, 8, 128).transpose(0, 1, 3, 2, 4)
    return out.reshape(2, 32, 2048)


def solution(mesh):
    return jax.shard_map(
        shards,
        mesh=mesh,
        in_specs=(
            P("tm", "space", None),
            P("space", None),
            P("space", None),
            P(None, "space", None),
            P("space", None),
            P("space", None),
        ),
        out_specs=P("tm", "space", None),
        check_vma=False,
    )
```

```python
import functools

import jax
import jax.numpy as jnp
from jax import lax
from jax.experimental import pallas as pl
from jax.experimental.pallas import tpu as pltpu
from jax.sharding import PartitionSpec as P

MESH = pl.DeviceIdType.MESH
F32 = jnp.float32

OFF = 16
ROWS = 64
MAIN = 32
COARSEN = 8
HALO = 12
TILE = 128


NSEM = 64


def kernel(
    cg, init, dif, vel, rea, src,
    out,
    st, co, cc, edges_in, fc, fcx, v, prev,
    lsem, ssem, rsem, esend, erecv, csend, crecv, xsend, xrecv, fsend, frecv, isend, irecv,
    *lev,
):
    t = lax.axis_index("tm")
    s = lax.axis_index("space")
    t_last, s_last = lax.axis_size("tm") - 1, lax.axis_size("space") - 1
    z_last = t_last // 2
    z, core = t // 2, t % 2
    odd = s % 2 == 1
    has_up, has_dn = s > 0, s < s_last
    double = z >= 5
    single = z < 5
    exports = (z >= 4) & (z < z_last)
    lead = z < z_last - 1
    skips = lead & (z >= 3)
    forks = z == 3
    passes = z <= 3
    origin = t == t_last

    lane = lax.broadcasted_iota(jnp.int32, (8, 128), 1)
    first_lane, last_lane = lane == 0, lane == 127

    loads = [
        (None, dif, st.at[0, pl.ds(2 * TILE, 512)]),
        (None, vel, st.at[pl.ds(1, 2), pl.ds(2 * TILE, 512)]),
        (None, rea, st.at[3, pl.ds(2 * TILE, 512)]),
        (None, src, st.at[4, pl.ds(2 * TILE, 512)]),
        (t < t_last, cg.at[0], st.at[5, pl.ds(2 * TILE, 512)]),
        (t < t_last, cg.at[1], st.at[6, pl.ds(2 * TILE, 512)]),
        (origin, init, st.at[5, pl.ds(2 * TILE, 512)]),
    ]

    def when(cond, body):
        if cond is None:
            body()
        else:
            pl.when(cond)(body)

    for i, (cond, a, b) in enumerate(loads):
        when(cond, lambda a=a, b=b, i=i: pltpu.make_async_copy(a, b, lsem.at[i]).start())

    zero = jnp.zeros((8, 128), F32)

    def clear(at_stage, rows):
        def body(i, _):
            for q in range(7):
                st[q, pl.ds(at_stage + i * 8, 8), :] = zero
            return 0

        lax.fori_loop(0, 32, body, 0)

        def rows_body(i, _):
            for f in range(2):
                for h in range(2):
                    edges_in[f, (0 if rows < 0 else HALO) + i, h] = zero
            for h in range(2):
                v[0, OFF + rows + i, h] = zero
                for q in range(4):
                    fcx[q, OFF + rows + i, h] = zero
            return 0

        lax.fori_loop(0, HALO, rows_body, 0)

    pl.when(s == 0)(lambda: clear(0, -HALO))
    pl.when(s == s_last)(lambda: clear(6 * TILE, MAIN))

    partners = []

    def partner(ok, pt, ps):
        partners.append((ok & (ps >= 0) & (ps <= s_last), pt, ps))

    for ds in (-1, 1):
        partner(t >= 0, t, s + ds)
    for ds in (-1, 0, 1):
        partner((core == 0) & (z > 0), t - 2, s + ds)
        partner((core == 0) & (z < z_last), t + 2, s + ds)
        partner((core == 0) & skips, t + 4, s + ds)
        partner((core == 0) & double, t - 4, s + ds)
    for ds in (-1, 1):
        partner((core == 1) & exports, t + 1, s + ds)
        partner((core == 0) & double, t - 1, s + ds)
    partner(t > 0, t - 1, s)
    partner(t < t_last, t + 1, s)
    partner((t == 0) | origin, t_last - t, s)
    barrier = pltpu.get_barrier_semaphore()
    count = 0
    for ok, pt, ps in partners:
        @pl.when(ok)
        def _(pt=pt, ps=ps):
            pl.semaphore_signal(barrier, inc=1, device_id=(pt, ps), device_id_type=MESH)
        count = count + ok.astype(jnp.int32)

    pl.semaphore_wait(barrier, count)

    used = [0]

    def remote(source, dest, device, sends, receives):
        i = used[0]
        used[0] += 1
        cp = pltpu.make_async_remote_copy(
            src_ref=source, dst_ref=dest, send_sem=ssem.at[i], recv_sem=rsem.at[i],
            device_id=device, device_id_type=MESH,
        )
        return sends, receives, cp

    def start(copies):
        for sends, _, cp in copies:
            pl.when(sends)(lambda cp=cp: cp.start())

    def wait_recv(copies):
        for _, receives, cp in copies:
            pl.when(receives)(lambda cp=cp: cp.wait_recv())

    def wait_send(copies):
        for sends, _, cp in copies:
            pl.when(sends)(lambda cp=cp: cp.wait_send())

    near, far, near_on, far_on = [], [], [], []
    half = pl.multiple_of(core * (TILE // 2), TILE // 2)
    sibling = (t + 1 - 2 * core, s)
    for group, onward, up_from, up_to, dn_from, dn_to in (
        (near, near_on, 3 * TILE, 1 * TILE, 0, 6 * TILE),
        (far, far_on, 2 * TILE, 0, TILE, 7 * TILE),
    ):
        for a, b in ((dif, 0), (vel, None), (rea, 3), (src, 4)):
            def part(at, a=a):
                rows = pl.ds(at + half, TILE // 2)
                return a.at[:, rows] if len(a.shape) == 3 else a.at[rows]

            def stage(at, b=b):
                rows = pl.ds(at + half, TILE // 2)
                return st.at[pl.ds(1, 2), rows] if b is None else st.at[b, rows]

            group.append(remote(part(up_from), stage(up_to), (t, s + 1), has_dn, has_up))
            group.append(remote(part(dn_from), stage(dn_to), (t, s - 1), has_up, has_dn))
            onward.append(remote(stage(up_to), stage(up_to), sibling, has_up, has_up))
            onward.append(remote(stage(dn_to), stage(dn_to), sibling, has_dn, has_dn))
    fields = []
    for a, b, mine in ((cg.at[0], 5, t < t_last), (cg.at[1], 6, t < t_last), (init, 5, origin)):
        fields += [
            remote(a.at[pl.ds(3 * TILE, TILE)], st.at[b, pl.ds(TILE, TILE)], (t, s + 1), mine & has_dn, mine & has_up),
            remote(a.at[pl.ds(0, TILE)], st.at[b, pl.ds(6 * TILE, TILE)], (t, s - 1), mine & has_up, mine & has_dn),
        ]
    start(near)
    start(fields)
    start(far)

    def staged(q, tile, r8, h):
        return st[q, pl.ds(tile * TILE + r8 + 8 * h, 8, stride=16), :]

    def coefficients(tile_lo, tiles):
        def body(i, _):
            tile = tile_lo + i
            for r8 in range(8):
                row = tile * 8 + r8
                for h in range(2):
                    d, b, c, k, sr = [staged(q, tile, r8, h) for q in range(5)]
                    u = d + jnp.maximum(b, 0.0)
                    n = d - jnp.minimum(b, 0.0)
                    le = d + jnp.maximum(c, 0.0)
                    ri = d - jnp.minimum(c, 0.0)
                    a = k - ((u + n) + (le + ri))
                    co[0, row, h] = 1.0 + a
                    co[1, row, h] = k
                    co[2, row, h] = u
                    co[3, row, h] = n
                    co[4, row, h] = le
                    co[5, row, h] = ri
                    co[6, row, h] = sr
            return 0

        lax.fori_loop(0, tiles, body, 0)

    def coarse_coefficients():
        def body(i, _):
            for j in range(4):
                row = OFF - 8 + i * 4 + j
                for h in range(2):
                    k, u, n, le, ri, sr = [8.0 * co[q, row, h] for q in range(1, 7)]
                    cc[0, row, h] = 1.0 + (k - ((u + n) + (le + ri)))
                    for q, x in enumerate((k, u, n, le, ri, sr)):
                        cc[1 + q, row, h] = x
            return 0

        lax.fori_loop(0, 12, body, 0)

    def field(q, dest, tile_lo, tiles):
        def body(i, _):
            tile = tile_lo + i
            for r8 in range(8):
                for h in range(2):
                    lev[0][dest, tile * 8 + r8, h] = staged(q, tile, r8, h)
            return 0

        lax.fori_loop(0, tiles, body, 0)

    def sides(a, b):
        ra, rb = pltpu.roll(a, 1, 1), pltpu.roll(b, 1, 1)
        la = jnp.where(first_lane, pltpu.roll(rb, 1, 0), ra)
        lb = jnp.where(first_lane, ra, rb)
        qa, qb = pltpu.roll(a, 127, 1), pltpu.roll(b, 127, 1)
        ga = jnp.where(last_lane, qb, qa)
        gb = jnp.where(last_lane, pltpu.roll(qa, 7, 0), qb)
        return (la, lb), (ga, gb)

    def step(state, coef, base, n, emit):
        load = lambda row: [state[row, h] for h in range(2)]
        up, ce = load(base - 1), load(base)
        for r in range(n):
            row = base + r
            dn = load(row + 1)
            left, right = sides(*ce)
            for h in range(2):
                a, k, u, d, le, ri, sr = [coef[q, row, h] for q in range(7)]
                x = ce[h]
                y = x * (a - k * (x * x)) + sr
                y = y + u * up[h] + d * dn[h]
                y = y + le * left[h] + ri * right[h]
                emit(r, row, h, y, x)
            up, ce = ce, dn

    for i, (cond, a, b) in enumerate(loads):
        when(cond, lambda a=a, b=b, i=i: pltpu.make_async_copy(a, b, lsem.at[i]).wait())
    coefficients(2, 4)
    field(5, 0, 2, 4)
    field(6, 1, 2, 4)

    def edge(f, side):
        from_row, to_row = ((OFF + MAIN - HALO, 0), (OFF, HALO))[side]
        return pltpu.make_async_remote_copy(
            src_ref=lev[0].at[f, pl.ds(from_row, HALO)], dst_ref=edges_in.at[f, pl.ds(to_row, HALO)],
            send_sem=esend.at[2 * f + side], recv_sem=erecv.at[2 * f + side],
            device_id=(t, s + 1 - 2 * side), device_id_type=MESH,
        )

    def chunk_row(m):
        return OFF + jnp.where(odd, 4 * m, 28 - 4 * m)

    def each_chunk(body):
        def one(m, _):
            body(m)
            return 0

        lax.fori_loop(0, 8, one, 0)

    def first_copy(m):
        rows = pl.ds(chunk_row(m), 4)
        return pltpu.make_async_remote_copy(
            src_ref=lev[0].at[0, rows], dst_ref=prev.at[rows], send_sem=fsend.at[m], recv_sem=frecv.at[m],
            device_id=(0, s), device_id_type=MESH,
        )

    n_fields = jnp.where(origin, 1, 2)

    def fine(f, k, base, n):
        def emit(r, row, h, y, x):
            lev[k][f, row, h] = y
            if k == COARSEN:
                fc[2 * core + f, row, h] = y - (8.0 * lev[1][f, row, h] - 7.0 * lev[0][f, row, h])

        step(lev[k - 1].at[f], co, base, n, emit)

    def interior(f, _):
        for k in range(1, COARSEN + 1):
            fine(f, k, OFF + k, MAIN - 2 * k)
        return 0

    def wedges(f, width):
        for k in range(1, COARSEN + 1):
            fine(f, k, OFF - width + k, width)
            fine(f, k, OFF + MAIN - k, width)

    def first_edges(f, _):
        wedges(f, COARSEN)
        for r in range(MAIN):
            for h in range(2):
                lev[0][f, OFF + r, h] = lev[COARSEN][f, OFF + r, h]
        pl.when(has_dn)(lambda: edge(f, 0).start())
        pl.when(has_up)(lambda: edge(f, 1).start())
        return 0

    def second_edges(f, _):
        pl.when(has_up)(lambda: edge(f, 0).wait_recv())
        pl.when(has_dn)(lambda: edge(f, 1).wait_recv())
        for r in range(HALO):
            for h in range(2):
                lev[0][f, OFF - HALO + r, h] = edges_in[f, r, h]
                lev[0][f, OFF + MAIN + r, h] = edges_in[f, HALO + r, h]
        wedges(f, HALO)
        return 0

    def relaxation(turn, _):
        lax.fori_loop(0, n_fields, interior, 0)

        @pl.when(turn == 0)
        def _():
            wait_recv(near)
            start(near_on)
            wait_recv(fields)
            for q in range(2):
                field(5 + q, q, 1, 1)
                field(5 + q, q, 6, 1)
            wait_recv(near_on)
            coefficients(1, 1)
            coefficients(6, 1)
            lax.fori_loop(0, n_fields, first_edges, 0)
            pl.when(origin)(lambda: each_chunk(lambda m: first_copy(m).start()))
            wait_recv(far)
            start(far_on)

        @pl.when(turn == 1)
        def _():
            wait_recv(far_on)
            coefficients(0, 1)
            coefficients(7, 1)
            coarse_coefficients()
            lax.fori_loop(0, n_fields, second_edges, 0)

        return 0

    lax.fori_loop(0, 2, relaxation, 0)

    give_f = [
        remote(fc.at[pl.ds(2, 2), pl.ds(OFF - 4, 40)], fc.at[pl.ds(2, 2), pl.ds(OFF - 4, 40)], (t - 1, s), (core == 1) & lead, (core == 0) & lead),
    ]
    start(give_f)

    def send_ahead(kind):
        from_row, to_row, n, ds = (
            (OFF - 4, OFF - 4, 40, 0), (OFF + MAIN - 8, OFF - 8, 4, 1), (OFF + 4, OFF + MAIN + 4, 4, -1),
        )[kind]
        fields = pl.ds(2 * core, 2)
        return pltpu.make_async_remote_copy(
            src_ref=fc.at[fields, pl.ds(from_row, n)], dst_ref=fcx.at[fields, pl.ds(to_row, n)],
            send_sem=isend.at[kind], recv_sem=irecv.at[3 * core + kind],
            device_id=(t + 2 - core, s + ds), device_id_type=MESH,
        )

    def arrive_ahead(c, kind):
        n = (40, 4, 4)[kind]
        rows = fcx.at[pl.ds(2 * c, 2), pl.ds(OFF - 4, n)]
        return pltpu.make_async_remote_copy(
            src_ref=rows, dst_ref=rows, send_sem=isend.at[kind], recv_sem=irecv.at[3 * c + kind],
            device_id=(t, s), device_id_type=MESH,
        )

    @pl.when(exports)
    def _():
        send_ahead(0).start()
        pl.when(has_dn)(lambda: send_ahead(1).start())
        pl.when(has_up)(lambda: send_ahead(2).start())

    def main_copy(top, hop, m, later=0):
        rows = pl.ds(chunk_row(m), 4)
        return pltpu.make_async_remote_copy(
            src_ref=v.at[top, rows], dst_ref=v.at[0, rows], send_sem=csend.at[later + m], recv_sem=crecv.at[m + 2],
            device_id=(t + 2 * hop, s), device_id_type=MESH,
        )

    inward = jnp.where(odd, -1, 1)

    def edge_copy(top, hop, m, later=0):
        there = jnp.where(m < 4, -1 - m, 15 - m)
        to_row = OFF + jnp.where(odd, 28 - 4 * there, 4 * there)
        return pltpu.make_async_remote_copy(
            src_ref=v.at[top, pl.ds(chunk_row(m), 4)], dst_ref=v.at[0, pl.ds(to_row, 4)],
            send_sem=csend.at[later + 8 + jnp.where(m < 4, m, m - 4)], recv_sem=crecv.at[there + 2],
            device_id=(t + 2 * hop, s + jnp.where(m < 4, inward, -inward)), device_id_type=MESH,
        )

    def arrived(slot):
        rows = v.at[0, pl.ds(OFF, 4)]
        return pltpu.make_async_remote_copy(
            src_ref=rows, dst_ref=rows, send_sem=csend.at[0], recv_sem=crecv.at[slot],
            device_id=(t, s), device_id_type=MESH,
        )

    def origin_copy(m):
        rows = pl.ds(chunk_row(m), 4)
        return pltpu.make_async_remote_copy(
            src_ref=lev[COARSEN].at[0, rows], dst_ref=v.at[0, rows], send_sem=csend.at[m + 2], recv_sem=crecv.at[m + 2],
            device_id=(0, s), device_id_type=MESH,
        )

    end_edge = jnp.where(odd, has_dn, has_up)

    @pl.when(origin)
    def _():
        origin_copy(-1).start()
        each_chunk(lambda m: origin_copy(m).start())
        pl.when(end_edge)(lambda: origin_copy(8).start())

    def give_copy(m, low=1):
        rows = pl.ds(chunk_row(m), 4)
        return pltpu.make_async_remote_copy(
            src_ref=v.at[pl.ds(low, 2), rows], dst_ref=v.at[pl.ds(1, 2), rows],
            send_sem=xsend.at[m], recv_sem=xrecv.at[m], device_id=(t + 1, s), device_id_type=MESH,
        )

    def onward_copy(m):
        rows = pl.ds(chunk_row(m), 4)
        return pltpu.make_async_remote_copy(
            src_ref=v.at[3, rows], dst_ref=prev.at[rows], send_sem=fsend.at[m], recv_sem=frecv.at[m],
            device_id=(t + 2, s), device_id_type=MESH,
        )

    def to_out(state, o, row):
        tile = (row - OFF) // 8
        r8 = (row - OFF) % 8
        for h in range(2):
            out[o, pl.ds(tile * TILE + r8 + 8 * h, 8, stride=16), :] = state[row, h]

    def state_out(top, hop, m, deep, act, later=0):
        at_start = (m == 0) | (deep & (m == 1))
        at_end = (m == 7) | (deep & (m == 6))
        pl.when(at_start | (at_end & end_edge))(lambda: act(edge_copy(top, hop, m, later)))
        act(main_copy(top, hop, m, later))

    def begin(copy):
        copy.start()

    def left(copy):
        copy.wait_send()

    no = t < 0
    hop = jnp.where(skips, 2, 1)

    def second_target(top, act):
        pl.when(forks)(lambda: each_chunk(lambda m: state_out(top, 1, m, no, act, 12)))

    def level(k, coarse_forcing, base, n):
        def emit(r, row, h, y, x):
            v[k, row, h] = y + coarse_forcing[row, h]

        step(v.at[k - 1], cc, base, n, emit)

    def chain_single():
        wait_recv(give_f)

        def base_of(i, k):
            return OFF + jnp.where(odd, 4 * i - 4 - k, 32 - 4 * i + k)

        def turn(i, _):
            pl.when(i == 1)(lambda: arrived(1).wait_recv())
            pl.when((i < 9) | end_edge)(lambda: arrived(i + 1).wait_recv())
            pl.when(i == 1)(lambda: level(1, fc.at[0], OFF + jnp.where(odd, -5, 29), 8))
            pl.when(i > 1)(lambda: level(1, fc.at[0], base_of(i, 1), 4))
            level(2, fc.at[1], base_of(i, 2), 4)
            m = i - 2

            @pl.when(lead)
            def _():
                level(3, fc.at[2], base_of(i, 3), 4)

                @pl.when(i > 1)
                def _():
                    level(4, fc.at[3], base_of(i, 4), 4)
                    state_out(4, hop, m, skips, begin)

            pl.when(i > 1)(lambda: give_copy(m).start())
            return 0

        lax.fori_loop(1, 10, turn, 0)
        second_target(4, begin)
        pl.when(passes)(lambda: each_chunk(lambda m: onward_copy(m).start()))

    def chain_double():
        for c in range(2):
            arrive_ahead(c, 0).wait_recv()
            pl.when(has_up)(lambda c=c: arrive_ahead(c, 1).wait_recv())
            pl.when(has_dn)(lambda c=c: arrive_ahead(c, 2).wait_recv())
        wait_recv(give_f)

        def one(j, k):
            level(k, fcx.at[k - 1] if k <= 4 else fc.at[k - 5], jnp.where(odd, 8 * j + (OFF - 8 - k), (OFF + 32 + k) - 8 * j), 8)

        def turn(j, _):
            for i in range(2):
                pl.when((j < 5) | end_edge)(lambda i=i: arrived(2 * j + i).wait_recv())
            for k in (1, 2, 3):
                one(j, k)

            @pl.when(j >= 1)
            def _():
                for k in (4, 5, 6):
                    one(j, k)

                @pl.when(lead)
                def _():
                    one(j, 7)
                    pl.when(j >= 2)(lambda: one(j, 8))

            @pl.when(j >= 2)
            def _():
                for i in range(2):
                    m = 2 * (j - 2) + i
                    pl.when(lead)(lambda m=m: state_out(8, hop, m, skips, begin))
                    give_copy(m, 5).start()

            return 0

        lax.fori_loop(0, 6, turn, 0)

    def finish_first():
        def body(m):
            onward_copy(m).wait_recv()
            for j in range(4):
                to_out(prev, 0, chunk_row(m) + j)
                to_out(v.at[0], 1, chunk_row(m) + j)

        each_chunk(body)

    def finish_double():
        def body(m):
            for j in range(4):
                to_out(v.at[3], 0, chunk_row(m) + j)
                to_out(v.at[4], 1, chunk_row(m) + j)

        each_chunk(body)

    def finish_second():
        def body(m):
            give_copy(m).wait_recv()
            for j in range(4):
                to_out(v.at[1], 0, chunk_row(m) + j)
                to_out(v.at[2], 1, chunk_row(m) + j)

        each_chunk(body)

    @pl.when((core == 0) & single)
    def _():
        chain_single()
        finish_first()

    @pl.when((core == 0) & double)
    def _():
        chain_double()
        finish_double()

    pl.when(core == 1)(finish_second)

    wait_send(near + far + near_on + far_on + fields + give_f)

    def edges_left(f, _):
        pl.when(has_dn)(lambda: edge(f, 0).wait_send())
        pl.when(has_up)(lambda: edge(f, 1).wait_send())
        return 0

    lax.fori_loop(0, n_fields, edges_left, 0)

    def drain(top, low):
        def body(m):
            pl.when(lead)(lambda: state_out(top, hop, m, skips, left))
            give_copy(m, low).wait_send()

        each_chunk(body)

    @pl.when((core == 0) & single)
    def _():
        drain(4, 1)
        second_target(4, left)
        pl.when(passes)(lambda: each_chunk(lambda m: onward_copy(m).wait_send()))

    pl.when((core == 0) & double)(lambda: drain(8, 5))

    @pl.when(exports)
    def _():
        send_ahead(0).wait_send()
        pl.when(has_dn)(lambda: send_ahead(1).wait_send())
        pl.when(has_up)(lambda: send_ahead(2).wait_send())

    @pl.when(origin)
    def _():
        def drain_origin(m):
            first_copy(m).wait_send()
            origin_copy(m).wait_send()

        each_chunk(drain_origin)
        origin_copy(-1).wait_send()
        pl.when(end_edge)(lambda: origin_copy(8).wait_send())


def tiles(x):
    lead = x.shape[:-2]
    n = len(lead)
    y = x.reshape(lead + (4, 8, 16, 128))
    y = y.transpose(tuple(range(n)) + (n, n + 2, n + 1, n + 3))
    return y.reshape(lead + (512, 128))


def shards(coarse_guess, initial, diffusion, velocity, reaction, source):
    hbm = pl.BlockSpec(memory_space=pltpu.HBM)
    state = (2, 8, 128)
    out = pl.pallas_call(
        kernel,
        out_shape=pltpu.VMEM((2, 512, 128), F32),
        in_specs=[hbm] * 6,
        out_specs=pl.BlockSpec(memory_space=pltpu.VMEM),
        scratch_shapes=[
            pltpu.VMEM((7, 8 * TILE, 128), F32),
            pltpu.VMEM((7, ROWS) + state, F32),
            pltpu.VMEM((7, ROWS) + state, F32),
            pltpu.VMEM((2, 2 * HALO) + state, F32),
            pltpu.VMEM((4, ROWS) + state, F32),
            pltpu.VMEM((4, ROWS) + state, F32),
            pltpu.VMEM((9, ROWS) + state, F32),
            pltpu.VMEM((ROWS,) + state, F32),
            pltpu.SemaphoreType.DMA((8,)),
            pltpu.SemaphoreType.DMA((NSEM,)),
            pltpu.SemaphoreType.DMA((NSEM,)),
            pltpu.SemaphoreType.DMA((4,)),
            pltpu.SemaphoreType.DMA((4,)),
            pltpu.SemaphoreType.DMA((24,)),
            pltpu.SemaphoreType.DMA((12,)),
            pltpu.SemaphoreType.DMA((8,)),
            pltpu.SemaphoreType.DMA((8,)),
            pltpu.SemaphoreType.DMA((8,)),
            pltpu.SemaphoreType.DMA((8,)),
            pltpu.SemaphoreType.DMA((3,)),
            pltpu.SemaphoreType.DMA((6,)),
        ] + [pltpu.VMEM((2, ROWS) + state, F32)] * (COARSEN + 1),
        compiler_params=pltpu.CompilerParams(
            collective_id=0, has_side_effects=True, vmem_limit_bytes=62 * 2**20
        ),
    )(tiles(coarse_guess), tiles(initial), tiles(diffusion), tiles(velocity), tiles(reaction), tiles(source))
    out = out.reshape(2, 4, 16, 8, 128).transpose(0, 1, 3, 2, 4)
    return out.reshape(2, 32, 2048)


def solution(mesh):
    return jax.shard_map(
        shards,
        mesh=mesh,
        in_specs=(
            P("tm", "space", None),
            P("space", None),
            P("space", None),
            P(None, "space", None),
            P("space", None),
            P("space", None),
        ),
        out_specs=P("tm", "space", None),
        check_vma=False,
    )
```

```python
import functools

import jax
import jax.numpy as jnp
from jax import lax
from jax.experimental import pallas as pl
from jax.experimental.pallas import tpu as pltpu
from jax.sharding import PartitionSpec as P

MESH = pl.DeviceIdType.MESH
F32 = jnp.float32

OFF = 16
ROWS = 64
MAIN = 32
COARSEN = 8
HALO = 12
TILE = 128


NSEM = 64


def kernel(
    cg, init, dif, vel, rea, src,
    out,
    st, co, cc, edges_in, fc, fcx, v,
    lsem, ssem, rsem, esend, erecv, csend, crecv, xsend, xrecv, isend, irecv, gsend, grecv,
    *lev,
):
    t = lax.axis_index("tm")
    s = lax.axis_index("space")
    t_last, s_last = lax.axis_size("tm") - 1, lax.axis_size("space") - 1
    z_last = t_last // 2
    z, core = t // 2, t % 2
    odd = s % 2 == 1
    has_up, has_dn = s > 0, s < s_last
    double = z >= 5
    single = z < 5
    exports = (z >= 4) & (z < z_last)
    lead = z < z_last - 1
    skips = lead & (z >= 3)
    forks = z == 3
    ends = t == t_last

    lane = lax.broadcasted_iota(jnp.int32, (8, 128), 1)
    first_lane, last_lane = lane == 0, lane == 127

    loads = [
        (None, dif, st.at[0, pl.ds(2 * TILE, 512)]),
        (None, vel, st.at[pl.ds(1, 2), pl.ds(2 * TILE, 512)]),
        (None, rea, st.at[3, pl.ds(2 * TILE, 512)]),
        (None, src, st.at[4, pl.ds(2 * TILE, 512)]),
        (t < t_last, cg.at[0], st.at[6, pl.ds(2 * TILE, 512)]),
        (t == 0, init, st.at[5, pl.ds(2 * TILE, 512)]),
    ]

    def when(cond, body):
        if cond is None:
            body()
        else:
            pl.when(cond)(body)

    for i, (cond, a, b) in enumerate(loads):
        when(cond, lambda a=a, b=b, i=i: pltpu.make_async_copy(a, b, lsem.at[i]).start())

    zero = jnp.zeros((8, 128), F32)

    def clear(at_stage, rows):
        def body(i, _):
            for q in range(7):
                st[q, pl.ds(at_stage + i * 8, 8), :] = zero
            return 0

        lax.fori_loop(0, 32, body, 0)

        def rows_body(i, _):
            for f in range(2):
                for h in range(2):
                    edges_in[f, (0 if rows < 0 else HALO) + i, h] = zero
            for h in range(2):
                v[0, OFF + rows + i, h] = zero
                for q in range(4):
                    fcx[q, OFF + rows + i, h] = zero
            return 0

        lax.fori_loop(0, HALO, rows_body, 0)

    pl.when(s == 0)(lambda: clear(0, -HALO))
    pl.when(s == s_last)(lambda: clear(6 * TILE, MAIN))

    partners = []

    def partner(ok, pt, ps):
        partners.append((ok & (ps >= 0) & (ps <= s_last), pt, ps))

    for ds in (-1, 1):
        partner(t >= 0, t, s + ds)
    for ds in (-1, 0, 1):
        partner((core == 0) & (z > 0), t - 2, s + ds)
        partner((core == 0) & (z < z_last), t + 2, s + ds)
        partner((core == 0) & skips, t + 4, s + ds)
        partner((core == 0) & double, t - 4, s + ds)
        partner(t < t_last, t + 1, s + ds)
        partner(t > 0, t - 1, s + ds)
    barrier = pltpu.get_barrier_semaphore()
    count = 0
    for ok, pt, ps in partners:
        @pl.when(ok)
        def _(pt=pt, ps=ps):
            pl.semaphore_signal(barrier, inc=1, device_id=(pt, ps), device_id_type=MESH)
        count = count + ok.astype(jnp.int32)

    pl.semaphore_wait(barrier, count)

    used = [0]

    def remote(source, dest, device, sends, receives):
        i = used[0]
        used[0] += 1
        cp = pltpu.make_async_remote_copy(
            src_ref=source, dst_ref=dest, send_sem=ssem.at[i], recv_sem=rsem.at[i],
            device_id=device, device_id_type=MESH,
        )
        return sends, receives, cp

    def start(copies):
        for sends, _, cp in copies:
            pl.when(sends)(lambda cp=cp: cp.start())

    def wait_recv(copies):
        for _, receives, cp in copies:
            pl.when(receives)(lambda cp=cp: cp.wait_recv())

    def wait_send(copies):
        for sends, _, cp in copies:
            pl.when(sends)(lambda cp=cp: cp.wait_send())

    near, far, near_on, far_on = [], [], [], []
    half = pl.multiple_of(core * (TILE // 2), TILE // 2)
    sibling = (t + 1 - 2 * core, s)
    for group, onward, up_from, up_to, dn_from, dn_to in (
        (near, near_on, 3 * TILE, 1 * TILE, 0, 6 * TILE),
        (far, far_on, 2 * TILE, 0, TILE, 7 * TILE),
    ):
        for a, b in ((dif, 0), (vel, None), (rea, 3), (src, 4)):
            def part(at, a=a):
                rows = pl.ds(at + half, TILE // 2)
                return a.at[:, rows] if len(a.shape) == 3 else a.at[rows]

            def stage(at, b=b):
                rows = pl.ds(at + half, TILE // 2)
                return st.at[pl.ds(1, 2), rows] if b is None else st.at[b, rows]

            group.append(remote(part(up_from), stage(up_to), (t, s + 1), has_dn, has_up))
            group.append(remote(part(dn_from), stage(dn_to), (t, s - 1), has_up, has_dn))
            onward.append(remote(stage(up_to), stage(up_to), sibling, has_up, has_up))
            onward.append(remote(stage(dn_to), stage(dn_to), sibling, has_dn, has_dn))
    own = [
        remote(cg.at[0, pl.ds(3 * TILE, TILE)], st.at[6, pl.ds(TILE, TILE)], (t, s + 1), (t < t_last) & has_dn, (t < t_last) & has_up),
        remote(cg.at[0, pl.ds(0, TILE)], st.at[6, pl.ds(6 * TILE, TILE)], (t, s - 1), (t < t_last) & has_up, (t < t_last) & has_dn),
    ]
    shifted = [remote(cg.at[1], st.at[5, pl.ds(2 * TILE, 512)], (t + 1, s), t < t_last, t > 0)]
    shifted_edges = [
        remote(cg.at[1, pl.ds(3 * TILE, TILE)], st.at[5, pl.ds(TILE, TILE)], (t + 1, s + 1), (t < t_last) & has_dn, (t > 0) & has_up),
        remote(cg.at[1, pl.ds(0, TILE)], st.at[5, pl.ds(6 * TILE, TILE)], (t + 1, s - 1), (t < t_last) & has_up, (t > 0) & has_dn),
        remote(init.at[pl.ds(3 * TILE, TILE)], st.at[5, pl.ds(TILE, TILE)], (t, s + 1), (t == 0) & has_dn, (t == 0) & has_up),
        remote(init.at[pl.ds(0, TILE)], st.at[5, pl.ds(6 * TILE, TILE)], (t, s - 1), (t == 0) & has_up, (t == 0) & has_dn),
    ]
    fields = shifted + own + shifted_edges
    start(near)
    start(fields)

    def staged(q, tile, r8, h):
        return st[q, pl.ds(tile * TILE + r8 + 8 * h, 8, stride=16), :]

    def coefficients(tile_lo, tiles):
        def body(i, _):
            tile = tile_lo + i
            for r8 in range(8):
                row = tile * 8 + r8
                for h in range(2):
                    d, b, c, k, sr = [staged(q, tile, r8, h) for q in range(5)]
                    u = d + jnp.maximum(b, 0.0)
                    n = d - jnp.minimum(b, 0.0)
                    le = d + jnp.maximum(c, 0.0)
                    ri = d - jnp.minimum(c, 0.0)
                    a = k - ((u + n) + (le + ri))
                    co[0, row, h] = 1.0 + a
                    co[1, row, h] = k
                    co[2, row, h] = u
                    co[3, row, h] = n
                    co[4, row, h] = le
                    co[5, row, h] = ri
                    co[6, row, h] = sr
            return 0

        lax.fori_loop(0, tiles, body, 0)

    def coarse_coefficients():
        def body(i, _):
            for j in range(4):
                row = OFF - 8 + i * 4 + j
                for h in range(2):
                    k, u, n, le, ri, sr = [8.0 * co[q, row, h] for q in range(1, 7)]
                    cc[0, row, h] = 1.0 + (k - ((u + n) + (le + ri)))
                    for q, x in enumerate((k, u, n, le, ri, sr)):
                        cc[1 + q, row, h] = x
            return 0

        lax.fori_loop(0, 12, body, 0)

    def field(q, dest, tile_lo, tiles):
        def body(i, _):
            tile = tile_lo + i
            for r8 in range(8):
                for h in range(2):
                    lev[0][dest, tile * 8 + r8, h] = staged(q, tile, r8, h)
            return 0

        lax.fori_loop(0, tiles, body, 0)

    def sides(a, b):
        ra, rb = pltpu.roll(a, 1, 1), pltpu.roll(b, 1, 1)
        la = jnp.where(first_lane, pltpu.roll(rb, 1, 0), ra)
        lb = jnp.where(first_lane, ra, rb)
        qa, qb = pltpu.roll(a, 127, 1), pltpu.roll(b, 127, 1)
        ga = jnp.where(last_lane, qb, qa)
        gb = jnp.where(last_lane, pltpu.roll(qa, 7, 0), qb)
        return (la, lb), (ga, gb)

    def step(state, coef, base, n, emit):
        load = lambda row: [state[row, h] for h in range(2)]
        up, ce = load(base - 1), load(base)
        for r in range(n):
            row = base + r
            dn = load(row + 1)
            left, right = sides(*ce)
            for h in range(2):
                a, k, u, d, le, ri, sr = [coef[q, row, h] for q in range(7)]
                x = ce[h]
                y = x * (a - k * (x * x)) + sr
                y = y + u * up[h] + d * dn[h]
                y = y + le * left[h] + ri * right[h]
                emit(r, row, h, y, x)
            up, ce = ce, dn

    for i, (cond, a, b) in enumerate(loads):
        when(cond, lambda a=a, b=b, i=i: pltpu.make_async_copy(a, b, lsem.at[i]).wait())
    coefficients(2, 4)
    field(6, 1, 2, 4)

    def edge(f, side):
        from_row, to_row = ((OFF + MAIN - HALO, 0), (OFF, HALO))[side]
        return pltpu.make_async_remote_copy(
            src_ref=lev[0].at[f, pl.ds(from_row, HALO)], dst_ref=edges_in.at[f, pl.ds(to_row, HALO)],
            send_sem=esend.at[2 * f + side], recv_sem=erecv.at[2 * f + side],
            device_id=(t, s + 1 - 2 * side), device_id_type=MESH,
        )

    def chunk_row(m):
        return OFF + jnp.where(odd, 4 * m, 28 - 4 * m)

    def each_chunk(body):
        def one(m, _):
            body(m)
            return 0

        lax.fori_loop(0, 8, one, 0)

    n_fields = jnp.where(ends, 1, 2)

    def fine(f, k, base, n):
        def emit(r, row, h, y, x):
            lev[k][f, row, h] = y
            if k == COARSEN:
                fc[2 * core + f, row, h] = y - (8.0 * lev[1][f, row, h] - 7.0 * lev[0][f, row, h])

        step(lev[k - 1].at[f], co, base, n, emit)

    def interior(turn, i):
        f = n_fields - 1 - i

        @pl.when((turn == 0) & (f == 0))
        def _():
            wait_recv(shifted)
            field(5, 0, 2, 4)

        for k in range(1, COARSEN + 1):
            fine(f, k, OFF + k, MAIN - 2 * k)

    def wedges(f, width):
        for k in range(1, COARSEN + 1):
            fine(f, k, OFF - width + k, width)
            fine(f, k, OFF + MAIN - k, width)

    def first_edges(i, _):
        f = n_fields - 1 - i
        pl.when(f == 0)(lambda: wait_recv(shifted_edges))
        pl.when(f == 1)(lambda: wait_recv(own))
        for q in range(2):

            @pl.when(f == q)
            def _(q=q):
                field(5 + q, q, 1, 1)
                field(5 + q, q, 6, 1)

        wedges(f, COARSEN)
        for r in range(MAIN):
            for h in range(2):
                lev[0][f, OFF + r, h] = lev[COARSEN][f, OFF + r, h]
        pl.when(has_dn)(lambda: edge(f, 0).start())
        pl.when(has_up)(lambda: edge(f, 1).start())
        return 0

    def send_ahead(kind, f):
        from_row, to_row, n, ds = (
            (OFF - 4, OFF - 4, 40, 0), (OFF + MAIN - 8, OFF - 8, 4, 1), (OFF + 4, OFF + MAIN + 4, 4, -1),
        )[kind]
        which = 2 * core + f
        return pltpu.make_async_remote_copy(
            src_ref=fc.at[which, pl.ds(from_row, n)], dst_ref=fcx.at[which, pl.ds(to_row, n)],
            send_sem=isend.at[3 * f + kind], recv_sem=irecv.at[3 * which + kind],
            device_id=(t + 2 - core, s + ds), device_id_type=MESH,
        )

    def arrive_ahead(which):
        for kind, cond, n in ((0, None, 40), (1, has_up, 4), (2, has_dn, 4)):
            rows = fcx.at[which, pl.ds(OFF - 4, n)]
            copy = pltpu.make_async_remote_copy(
                src_ref=rows, dst_ref=rows, send_sem=isend.at[kind], recv_sem=irecv.at[3 * which + kind],
                device_id=(t, s), device_id_type=MESH,
            )
            when(cond, copy.wait_recv)

    def ahead(f, act):
        @pl.when(exports)
        def _():
            act(send_ahead(0, f))
            pl.when(has_dn)(lambda: act(send_ahead(1, f)))
            pl.when(has_up)(lambda: act(send_ahead(2, f)))

    def give_forcing(f):
        rows = fc.at[2 + f, pl.ds(OFF - 4, 40)]
        return pltpu.make_async_remote_copy(
            src_ref=rows, dst_ref=rows, send_sem=gsend.at[f], recv_sem=grecv.at[f],
            device_id=(t - 1, s), device_id_type=MESH,
        )

    def begin(copy):
        copy.start()

    def left(copy):
        copy.wait_send()

    def second_edges(i, _):
        f = n_fields - 1 - i
        pl.when(has_up)(lambda: edge(f, 0).wait_recv())
        pl.when(has_dn)(lambda: edge(f, 1).wait_recv())
        for r in range(HALO):
            for h in range(2):
                lev[0][f, OFF - HALO + r, h] = edges_in[f, r, h]
                lev[0][f, OFF + MAIN + r, h] = edges_in[f, HALO + r, h]
        wedges(f, HALO)
        pl.when(core == 1)(lambda: give_forcing(f).start())
        ahead(f, begin)
        return 0

    def relaxation(turn, _):
        def inner(i, _):
            interior(turn, i)
            return 0

        lax.fori_loop(0, n_fields, inner, 0)

        @pl.when(turn == 0)
        def _():
            wait_recv(near)
            start(near_on)
            start(far)
            wait_recv(near_on)
            coefficients(1, 1)
            coefficients(6, 1)
            lax.fori_loop(0, n_fields, first_edges, 0)
            wait_recv(far)
            start(far_on)

        @pl.when(turn == 1)
        def _():
            wait_recv(far_on)
            coefficients(0, 1)
            coefficients(7, 1)
            coarse_coefficients()
            lax.fori_loop(0, n_fields, second_edges, 0)

        return 0

    lax.fori_loop(0, 2, relaxation, 0)

    def main_copy(top, hop, m, later=0):
        rows = pl.ds(chunk_row(m), 4)
        return pltpu.make_async_remote_copy(
            src_ref=v.at[top, rows], dst_ref=v.at[0, rows], send_sem=csend.at[later + m], recv_sem=crecv.at[m + 2],
            device_id=(t + 2 * hop, s), device_id_type=MESH,
        )

    inward = jnp.where(odd, -1, 1)

    def edge_copy(top, hop, m, later=0):
        there = jnp.where(m < 4, -1 - m, 15 - m)
        to_row = OFF + jnp.where(odd, 28 - 4 * there, 4 * there)
        return pltpu.make_async_remote_copy(
            src_ref=v.at[top, pl.ds(chunk_row(m), 4)], dst_ref=v.at[0, pl.ds(to_row, 4)],
            send_sem=csend.at[later + 8 + jnp.where(m < 4, m, m - 4)], recv_sem=crecv.at[there + 2],
            device_id=(t + 2 * hop, s + jnp.where(m < 4, inward, -inward)), device_id_type=MESH,
        )

    def arrived(slot):
        rows = v.at[0, pl.ds(OFF, 4)]
        return pltpu.make_async_remote_copy(
            src_ref=rows, dst_ref=rows, send_sem=csend.at[0], recv_sem=crecv.at[slot],
            device_id=(t, s), device_id_type=MESH,
        )

    end_edge = jnp.where(odd, has_dn, has_up)

    def give_copy(low, j, n):
        rows = pl.ds(OFF + jnp.where(odd, 8 * j, MAIN - n - 8 * j), n)
        return pltpu.make_async_remote_copy(
            src_ref=v.at[pl.ds(low, 2), rows], dst_ref=v.at[pl.ds(1, 2), rows],
            send_sem=xsend.at[j], recv_sem=xrecv.at[j], device_id=(t + 1, s), device_id_type=MESH,
        )

    def to_out(state, o, row):
        tile = (row - OFF) // 8
        r8 = (row - OFF) % 8
        for h in range(2):
            out[o, pl.ds(tile * TILE + r8 + 8 * h, 8, stride=16), :] = state[row, h]

    def state_out(top, hop, m, deep, act, later=0):
        at_start = (m == 0) | (deep & (m == 1))
        at_end = (m == 7) | (deep & (m == 6))
        pl.when(at_start | (at_end & end_edge))(lambda: act(edge_copy(top, hop, m, later)))
        act(main_copy(top, hop, m, later))

    no = t < 0
    hop = jnp.where(skips, 2, 1)

    def second_target(top, act):
        pl.when(forks)(lambda: each_chunk(lambda m: state_out(top, 1, m, no, act, 12)))

    def level(k, coarse_forcing, base, n):
        def emit(r, row, h, y, x):
            v[k, row, h] = y + coarse_forcing[row, h]

        step(v.at[k - 1], cc, base, n, emit)

    def span(p, n, c=0):
        return jnp.where(odd, p + (OFF + c), (OFF + MAIN - n - c) - p)

    def chain_single():
        @pl.when(z == 0)
        def _():
            def body(i, _):
                for j in range(4):
                    row = OFF - 4 + 4 * i + j
                    for h in range(2):
                        v[0, row, h] = lev[0][0, row, h]
                        v[1, row, h] = lev[COARSEN][0, row, h]
                return 0

            lax.fori_loop(0, 10, body, 0)

        later = z > 0

        def turn(i, _):
            pl.when(later & (i == 1))(lambda: arrived(1).wait_recv())
            pl.when(later & ((i < 9) | end_edge))(lambda: arrived(i + 1).wait_recv())
            pl.when(later & (i == 1))(lambda: level(1, fc.at[0], span(0, 8, -5), 8))
            pl.when(later & (i > 1))(lambda: level(1, fc.at[0], span(4 * i, 4, -5), 4))
            level(2, fc.at[1], span(4 * i, 4, -6), 4)

            @pl.when(i == 1)
            def _():
                give_forcing(0).wait_recv()
                give_forcing(1).wait_recv()

            level(3, fc.at[2], span(4 * i, 4, -7), 4)

            @pl.when(i > 1)
            def _():
                level(4, fc.at[3], span(4 * i, 4, -8), 4)
                state_out(4, hop, i - 2, skips, begin)

            return 0

        lax.fori_loop(1, 10, turn, 0)
        give_copy(2, 0, MAIN).start()
        second_target(4, begin)

    def chain_double():
        def one(j, k):
            coarse_forcing = fcx.at[k - 1] if k <= 4 else fc.at[k - 5]
            level(k, coarse_forcing, span(8 * j, 8, -8 - k), 8)

        for which in range(4):
            arrive_ahead(which)
        give_forcing(0).wait_recv()
        pl.when(z < z_last)(lambda: give_forcing(1).wait_recv())

        def turn(j, _):
            for i in range(2):
                pl.when((j < 5) | end_edge)(lambda i=i: arrived(2 * j + i).wait_recv())
            for k in (1, 2, 3):
                one(j, k)

            @pl.when(j >= 1)
            def _():
                for k in (4, 5, 6, 7):
                    one(j, k)

            @pl.when(j >= 2)
            def _():
                @pl.when(lead)
                def _():
                    one(j, 8)
                    for i in range(2):
                        state_out(8, hop, 2 * (j - 2) + i, skips, begin)

                give_copy(6, j - 2, 8).start()

            return 0

        lax.fori_loop(0, 6, turn, 0)

    def finish_first(low):
        def body(j, _):
            for r in range(8):
                row = OFF + 8 * j + r
                to_out(v.at[low], 0, row)
                to_out(v.at[low + 1], 1, row)
            return 0

        lax.fori_loop(0, 4, body, 0)

    def finish_second():
        def rows(first, n):
            for r in range(n):
                to_out(v.at[1], 0, first + r)
                to_out(v.at[2], 1, first + r)

        def body(j, _):
            pl.when(double)(lambda: give_copy(6, j, 8).wait_recv())
            rows(span(8 * j, 8), 8)
            return 0

        pl.when(single)(lambda: give_copy(2, 0, MAIN).wait_recv())
        lax.fori_loop(0, 4, body, 0)

    @pl.when((core == 0) & single)
    def _():
        chain_single()
        finish_first(0)

    @pl.when((core == 0) & double)
    def _():
        chain_double()
        finish_first(4)

    pl.when(core == 1)(finish_second)

    wait_send(near + far + near_on + far_on + fields)

    def edges_left(f, _):
        pl.when(has_dn)(lambda: edge(f, 0).wait_send())
        pl.when(has_up)(lambda: edge(f, 1).wait_send())
        return 0

    lax.fori_loop(0, n_fields, edges_left, 0)

    def drain(top):
        def body(m):
            pl.when(lead)(lambda: state_out(top, hop, m, skips, left))

        each_chunk(body)

    @pl.when((core == 0) & single)
    def _():
        drain(4)
        give_copy(2, 0, MAIN).wait_send()
        second_target(4, left)

    @pl.when((core == 0) & double)
    def _():
        drain(8)
        for j in range(4):
            give_copy(6, j, 8).wait_send()


    def forcing_left(f, _):
        pl.when(core == 1)(lambda: give_forcing(f).wait_send())
        ahead(f, left)
        return 0

    lax.fori_loop(0, n_fields, forcing_left, 0)


def tiles(x):
    lead = x.shape[:-2]
    n = len(lead)
    y = x.reshape(lead + (4, 8, 16, 128))
    y = y.transpose(tuple(range(n)) + (n, n + 2, n + 1, n + 3))
    return y.reshape(lead + (512, 128))


def shards(coarse_guess, initial, diffusion, velocity, reaction, source):
    hbm = pl.BlockSpec(memory_space=pltpu.HBM)
    state = (2, 8, 128)
    out = pl.pallas_call(
        kernel,
        out_shape=pltpu.VMEM((2, 512, 128), F32),
        in_specs=[hbm] * 6,
        out_specs=pl.BlockSpec(memory_space=pltpu.VMEM),
        scratch_shapes=[
            pltpu.VMEM((7, 8 * TILE, 128), F32),
            pltpu.VMEM((7, ROWS) + state, F32),
            pltpu.VMEM((7, ROWS) + state, F32),
            pltpu.VMEM((2, 2 * HALO) + state, F32),
            pltpu.VMEM((4, ROWS) + state, F32),
            pltpu.VMEM((4, ROWS) + state, F32),
            pltpu.VMEM((9, ROWS) + state, F32),
            pltpu.SemaphoreType.DMA((8,)),
            pltpu.SemaphoreType.DMA((NSEM,)),
            pltpu.SemaphoreType.DMA((NSEM,)),
            pltpu.SemaphoreType.DMA((4,)),
            pltpu.SemaphoreType.DMA((4,)),
            pltpu.SemaphoreType.DMA((24,)),
            pltpu.SemaphoreType.DMA((12,)),
            pltpu.SemaphoreType.DMA((8,)),
            pltpu.SemaphoreType.DMA((8,)),
            pltpu.SemaphoreType.DMA((6,)),
            pltpu.SemaphoreType.DMA((12,)),
            pltpu.SemaphoreType.DMA((2,)),
            pltpu.SemaphoreType.DMA((2,)),
        ] + [pltpu.VMEM((2, ROWS) + state, F32)] * (COARSEN + 1),
        compiler_params=pltpu.CompilerParams(
            collective_id=0, has_side_effects=True, vmem_limit_bytes=62 * 2**20
        ),
    )(tiles(coarse_guess), tiles(initial), tiles(diffusion), tiles(velocity), tiles(reaction), tiles(source))
    out = out.reshape(2, 4, 16, 8, 128).transpose(0, 1, 3, 2, 4)
    return out.reshape(2, 32, 2048)


def solution(mesh):
    return jax.shard_map(
        shards,
        mesh=mesh,
        in_specs=(
            P("tm", "space", None),
            P("space", None),
            P("space", None),
            P(None, "space", None),
            P("space", None),
            P("space", None),
        ),
        out_specs=P("tm", "space", None),
        check_vma=False,
    )
```

```python
import functools

import jax
import jax.numpy as jnp
from jax import lax
from jax.experimental import pallas as pl
from jax.experimental.pallas import tpu as pltpu
from jax.sharding import PartitionSpec as P

MESH = pl.DeviceIdType.MESH
F32 = jnp.float32

OFF = 16
ROWS = 64
MAIN = 32
COARSEN = 8
HALO = 12
TILE = 128


NSEM = 64


def kernel(
    cg, init, dif, vel, rea, src,
    out,
    st, co, cc, edges_in, fc, fcx, v,
    lsem, ssem, rsem, esend, erecv, csend, crecv, xsend, xrecv, isend, irecv, gsend, grecv,
    *lev,
):
    t = lax.axis_index("tm")
    s = lax.axis_index("space")
    t_last, s_last = lax.axis_size("tm") - 1, lax.axis_size("space") - 1
    z_last = t_last // 2
    z, core = t // 2, t % 2
    odd = s % 2 == 1
    has_up, has_dn = s > 0, s < s_last
    double = z >= 5
    single = z < 5
    exports = (z >= 4) & (z < z_last)
    lead = z < z_last - 1
    skips = lead & (z >= 3)
    forks = z == 3
    ends = t == t_last

    lane = lax.broadcasted_iota(jnp.int32, (8, 128), 1)
    first_lane, last_lane = lane == 0, lane == 127

    loads = [
        (None, dif, st.at[0, pl.ds(2 * TILE, 512)]),
        (None, vel, st.at[pl.ds(1, 2), pl.ds(2 * TILE, 512)]),
        (None, rea, st.at[3, pl.ds(2 * TILE, 512)]),
        (None, src, st.at[4, pl.ds(2 * TILE, 512)]),
        (t < t_last, cg.at[0], st.at[6, pl.ds(2 * TILE, 512)]),
        (t == 0, init, st.at[5, pl.ds(2 * TILE, 512)]),
    ]

    def when(cond, body):
        if cond is None:
            body()
        else:
            pl.when(cond)(body)

    for i, (cond, a, b) in enumerate(loads):
        when(cond, lambda a=a, b=b, i=i: pltpu.make_async_copy(a, b, lsem.at[i]).start())

    zero = jnp.zeros((8, 128), F32)

    def clear(at_stage, rows):
        def body(i, _):
            for q in range(7):
                st[q, pl.ds(at_stage + i * 8, 8), :] = zero
            return 0

        lax.fori_loop(0, 32, body, 0)

        def rows_body(i, _):
            for f in range(2):
                for h in range(2):
                    edges_in[f, (0 if rows < 0 else HALO) + i, h] = zero
            for h in range(2):
                v[0, OFF + rows + i, h] = zero
                for q in range(4):
                    fcx[q, OFF + rows + i, h] = zero
            return 0

        lax.fori_loop(0, HALO, rows_body, 0)

    pl.when(s == 0)(lambda: clear(0, -HALO))
    pl.when(s == s_last)(lambda: clear(6 * TILE, MAIN))

    partners = []

    def partner(ok, pt, ps):
        partners.append((ok & (ps >= 0) & (ps <= s_last), pt, ps))

    for ds in (-1, 1):
        partner(t >= 0, t, s + ds)
    for ds in (-1, 0, 1):
        partner((core == 0) & (z > 0), t - 2, s + ds)
        partner((core == 0) & (z < z_last), t + 2, s + ds)
        partner((core == 0) & skips, t + 4, s + ds)
        partner((core == 0) & double, t - 4, s + ds)
        partner(t < t_last, t + 1, s + ds)
        partner(t > 0, t - 1, s + ds)
    barrier = pltpu.get_barrier_semaphore()
    count = 0
    for ok, pt, ps in partners:
        @pl.when(ok)
        def _(pt=pt, ps=ps):
            pl.semaphore_signal(barrier, inc=1, device_id=(pt, ps), device_id_type=MESH)
        count = count + ok.astype(jnp.int32)

    pl.semaphore_wait(barrier, count)

    used = [0]

    def remote(source, dest, device, sends, receives):
        i = used[0]
        used[0] += 1
        cp = pltpu.make_async_remote_copy(
            src_ref=source, dst_ref=dest, send_sem=ssem.at[i], recv_sem=rsem.at[i],
            device_id=device, device_id_type=MESH,
        )
        return sends, receives, cp

    def start(copies):
        for sends, _, cp in copies:
            pl.when(sends)(lambda cp=cp: cp.start())

    def wait_recv(copies):
        for _, receives, cp in copies:
            pl.when(receives)(lambda cp=cp: cp.wait_recv())

    def wait_send(copies):
        for sends, _, cp in copies:
            pl.when(sends)(lambda cp=cp: cp.wait_send())

    near, far, near_on, far_on = [], [], [], []
    half = pl.multiple_of(core * (TILE // 2), TILE // 2)
    sibling = (t + 1 - 2 * core, s)
    for group, onward, up_from, up_to, dn_from, dn_to in (
        (near, near_on, 3 * TILE, 1 * TILE, 0, 6 * TILE),
        (far, far_on, 2 * TILE, 0, TILE, 7 * TILE),
    ):
        for a, b in ((dif, 0), (vel, None), (rea, 3), (src, 4)):
            def part(at, a=a):
                rows = pl.ds(at + half, TILE // 2)
                return a.at[:, rows] if len(a.shape) == 3 else a.at[rows]

            def stage(at, b=b):
                rows = pl.ds(at + half, TILE // 2)
                return st.at[pl.ds(1, 2), rows] if b is None else st.at[b, rows]

            group.append(remote(part(up_from), stage(up_to), (t, s + 1), has_dn, has_up))
            group.append(remote(part(dn_from), stage(dn_to), (t, s - 1), has_up, has_dn))
            onward.append(remote(stage(up_to), stage(up_to), sibling, has_up, has_up))
            onward.append(remote(stage(dn_to), stage(dn_to), sibling, has_dn, has_dn))
    own = [
        remote(cg.at[0, pl.ds(3 * TILE, TILE)], st.at[6, pl.ds(TILE, TILE)], (t, s + 1), (t < t_last) & has_dn, (t < t_last) & has_up),
        remote(cg.at[0, pl.ds(0, TILE)], st.at[6, pl.ds(6 * TILE, TILE)], (t, s - 1), (t < t_last) & has_up, (t < t_last) & has_dn),
    ]
    shifted = [remote(cg.at[1], st.at[5, pl.ds(2 * TILE, 512)], (t + 1, s), t < t_last, t > 0)]
    shifted_edges = [
        remote(cg.at[1, pl.ds(3 * TILE, TILE)], st.at[5, pl.ds(TILE, TILE)], (t + 1, s + 1), (t < t_last) & has_dn, (t > 0) & has_up),
        remote(cg.at[1, pl.ds(0, TILE)], st.at[5, pl.ds(6 * TILE, TILE)], (t + 1, s - 1), (t < t_last) & has_up, (t > 0) & has_dn),
        remote(init.at[pl.ds(3 * TILE, TILE)], st.at[5, pl.ds(TILE, TILE)], (t, s + 1), (t == 0) & has_dn, (t == 0) & has_up),
        remote(init.at[pl.ds(0, TILE)], st.at[5, pl.ds(6 * TILE, TILE)], (t, s - 1), (t == 0) & has_up, (t == 0) & has_dn),
    ]
    fields = shifted + own + shifted_edges
    start(near)
    start(fields)

    def staged(q, tile, r8, h):
        return st[q, pl.ds(tile * TILE + r8 + 8 * h, 8, stride=16), :]

    def coefficients(tile_lo, tiles):
        def body(i, _):
            tile = tile_lo + i
            for r8 in range(8):
                row = tile * 8 + r8
                for h in range(2):
                    d, b, c, k, sr = [staged(q, tile, r8, h) for q in range(5)]
                    u = d + jnp.maximum(b, 0.0)
                    n = d - jnp.minimum(b, 0.0)
                    le = d + jnp.maximum(c, 0.0)
                    ri = d - jnp.minimum(c, 0.0)
                    a = k - ((u + n) + (le + ri))
                    co[0, row, h] = 1.0 + a
                    co[1, row, h] = k
                    co[2, row, h] = u
                    co[3, row, h] = n
                    co[4, row, h] = le
                    co[5, row, h] = ri
                    co[6, row, h] = sr
            return 0

        lax.fori_loop(0, tiles, body, 0)

    def coarse_coefficients():
        def body(i, _):
            for j in range(4):
                row = OFF - 8 + i * 4 + j
                for h in range(2):
                    k, u, n, le, ri, sr = [8.0 * co[q, row, h] for q in range(1, 7)]
                    cc[0, row, h] = 1.0 + (k - ((u + n) + (le + ri)))
                    for q, x in enumerate((k, u, n, le, ri, sr)):
                        cc[1 + q, row, h] = x
            return 0

        lax.fori_loop(0, 12, body, 0)

    def field(q, dest, tile_lo, tiles):
        def body(i, _):
            tile = tile_lo + i
            for r8 in range(8):
                for h in range(2):
                    lev[0][dest, tile * 8 + r8, h] = staged(q, tile, r8, h)
            return 0

        lax.fori_loop(0, tiles, body, 0)

    def sides(a, b):
        ra, rb = pltpu.roll(a, 1, 1), pltpu.roll(b, 1, 1)
        la = jnp.where(first_lane, pltpu.roll(rb, 1, 0), ra)
        lb = jnp.where(first_lane, ra, rb)
        qa, qb = pltpu.roll(a, 127, 1), pltpu.roll(b, 127, 1)
        ga = jnp.where(last_lane, qb, qa)
        gb = jnp.where(last_lane, pltpu.roll(qa, 7, 0), qb)
        return (la, lb), (ga, gb)

    def step(state, coef, base, n, emit):
        load = lambda row: [state[row, h] for h in range(2)]
        up, ce = load(base - 1), load(base)
        for r in range(n):
            row = base + r
            dn = load(row + 1)
            left, right = sides(*ce)
            for h in range(2):
                a, k, u, d, le, ri, sr = [coef[q, row, h] for q in range(7)]
                x = ce[h]
                y = x * (a - k * (x * x)) + sr
                y = y + u * up[h] + d * dn[h]
                y = y + le * left[h] + ri * right[h]
                emit(r, row, h, y, x)
            up, ce = ce, dn

    for i, (cond, a, b) in enumerate(loads):
        when(cond, lambda a=a, b=b, i=i: pltpu.make_async_copy(a, b, lsem.at[i]).wait())
    coefficients(2, 4)
    field(6, 1, 2, 4)

    def edge(f, side):
        from_row, to_row = ((OFF + MAIN - HALO, 0), (OFF, HALO))[side]
        return pltpu.make_async_remote_copy(
            src_ref=lev[0].at[f, pl.ds(from_row, HALO)], dst_ref=edges_in.at[f, pl.ds(to_row, HALO)],
            send_sem=esend.at[2 * f + side], recv_sem=erecv.at[2 * f + side],
            device_id=(t, s + 1 - 2 * side), device_id_type=MESH,
        )

    def chunk_row(m):
        return OFF + jnp.where(odd, 4 * m, 28 - 4 * m)

    def each_chunk(body):
        def one(m, _):
            body(m)
            return 0

        lax.fori_loop(0, 8, one, 0)

    n_fields = jnp.where(ends, 1, 2)

    def fine(f, k, base, n):
        def emit(r, row, h, y, x):
            lev[k][f, row, h] = y
            if k == COARSEN:
                fc[2 * core + f, row, h] = y - (8.0 * lev[1][f, row, h] - 7.0 * lev[0][f, row, h])

        step(lev[k - 1].at[f], co, base, n, emit)

    parts = (
        (OFF - 4, OFF - 4, 12, 0), (OFF + 24, OFF + 24, 12, 0), (OFF + 8, OFF + 8, 16, 0),
        (OFF + MAIN - 7, OFF - 7, 3, 1), (OFF + 4, OFF + MAIN + 4, 3, -1),
    )

    def send_ahead(part, f):
        from_row, to_row, n, ds = parts[part]
        which = 2 * core + f
        return pltpu.make_async_remote_copy(
            src_ref=fc.at[which, pl.ds(from_row, n)], dst_ref=fcx.at[which, pl.ds(to_row, n)],
            send_sem=isend.at[5 * f + part], recv_sem=irecv.at[5 * which + part],
            device_id=(t + 2 - core, s + ds), device_id_type=MESH,
        )

    def interior(turn, i):
        f = n_fields - 1 - i

        @pl.when((turn == 0) & (f == 0))
        def _():
            wait_recv(shifted)
            field(5, 0, 2, 4)

        for k in range(1, COARSEN + 1):
            fine(f, k, OFF + k, MAIN - 2 * k)
        pl.when(exports & (turn == 1))(lambda: send_ahead(2, f).start())

    def wedges(f, width):
        for k in range(1, COARSEN + 1):
            fine(f, k, OFF - width + k, width)
            fine(f, k, OFF + MAIN - k, width)

    def first_edges(i, _):
        f = n_fields - 1 - i
        pl.when(f == 0)(lambda: wait_recv(shifted_edges))
        pl.when(f == 1)(lambda: wait_recv(own))
        for q in range(2):

            @pl.when(f == q)
            def _(q=q):
                field(5 + q, q, 1, 1)
                field(5 + q, q, 6, 1)

        wedges(f, COARSEN)
        for r in range(MAIN):
            for h in range(2):
                lev[0][f, OFF + r, h] = lev[COARSEN][f, OFF + r, h]
        pl.when(has_dn)(lambda: edge(f, 0).start())
        pl.when(has_up)(lambda: edge(f, 1).start())
        return 0

    def arrive_ahead(which):
        conds = (None, None, None) + ((has_up, has_dn) if which < 3 else ())
        for part, cond in enumerate(conds):
            rows = fcx.at[which, pl.ds(OFF - 4, parts[part][2])]
            copy = pltpu.make_async_remote_copy(
                src_ref=rows, dst_ref=rows, send_sem=isend.at[part], recv_sem=irecv.at[5 * which + part],
                device_id=(t, s), device_id_type=MESH,
            )
            when(cond, copy.wait_recv)

    def ahead(f, act):
        @pl.when(exports)
        def _():
            act(send_ahead(0, f))
            act(send_ahead(1, f))
            beyond = 2 * core + f < 3
            pl.when(has_dn & beyond)(lambda: act(send_ahead(3, f)))
            pl.when(has_up & beyond)(lambda: act(send_ahead(4, f)))

    def give_forcing(f):
        rows = fc.at[2 + f, pl.ds(OFF - 4, 40)]
        return pltpu.make_async_remote_copy(
            src_ref=rows, dst_ref=rows, send_sem=gsend.at[f], recv_sem=grecv.at[f],
            device_id=(t - 1, s), device_id_type=MESH,
        )

    def begin(copy):
        copy.start()

    def left(copy):
        copy.wait_send()

    def second_edges(i, _):
        f = n_fields - 1 - i
        pl.when(has_up)(lambda: edge(f, 0).wait_recv())
        pl.when(has_dn)(lambda: edge(f, 1).wait_recv())
        for r in range(HALO):
            for h in range(2):
                lev[0][f, OFF - HALO + r, h] = edges_in[f, r, h]
                lev[0][f, OFF + MAIN + r, h] = edges_in[f, HALO + r, h]
        wedges(f, HALO)
        pl.when(core == 1)(lambda: give_forcing(f).start())
        ahead(f, begin)
        return 0

    def relaxation(turn, _):
        def inner(i, _):
            interior(turn, i)
            return 0

        lax.fori_loop(0, n_fields, inner, 0)

        @pl.when(turn == 0)
        def _():
            wait_recv(near)
            start(near_on)
            start(far)
            wait_recv(near_on)
            coefficients(1, 1)
            coefficients(6, 1)
            lax.fori_loop(0, n_fields, first_edges, 0)
            wait_recv(far)
            start(far_on)

        @pl.when(turn == 1)
        def _():
            wait_recv(far_on)
            coefficients(0, 1)
            coefficients(7, 1)
            coarse_coefficients()
            lax.fori_loop(0, n_fields, second_edges, 0)

        return 0

    lax.fori_loop(0, 2, relaxation, 0)

    def main_copy(top, hop, m, later=0):
        rows = pl.ds(chunk_row(m), 4)
        return pltpu.make_async_remote_copy(
            src_ref=v.at[top, rows], dst_ref=v.at[0, rows], send_sem=csend.at[later + m], recv_sem=crecv.at[m + 2],
            device_id=(t + 2 * hop, s), device_id_type=MESH,
        )

    inward = jnp.where(odd, -1, 1)

    def edge_copy(top, hop, m, later=0):
        there = jnp.where(m < 4, -1 - m, 15 - m)
        to_row = OFF + jnp.where(odd, 28 - 4 * there, 4 * there)
        return pltpu.make_async_remote_copy(
            src_ref=v.at[top, pl.ds(chunk_row(m), 4)], dst_ref=v.at[0, pl.ds(to_row, 4)],
            send_sem=csend.at[later + 8 + jnp.where(m < 4, m, m - 4)], recv_sem=crecv.at[there + 2],
            device_id=(t + 2 * hop, s + jnp.where(m < 4, inward, -inward)), device_id_type=MESH,
        )

    def arrived(slot):
        rows = v.at[0, pl.ds(OFF, 4)]
        return pltpu.make_async_remote_copy(
            src_ref=rows, dst_ref=rows, send_sem=csend.at[0], recv_sem=crecv.at[slot],
            device_id=(t, s), device_id_type=MESH,
        )

    end_edge = jnp.where(odd, has_dn, has_up)

    def give_copy(low, j, n):
        rows = pl.ds(OFF + jnp.where(odd, 8 * j, MAIN - n - 8 * j), n)
        return pltpu.make_async_remote_copy(
            src_ref=v.at[pl.ds(low, 2), rows], dst_ref=v.at[pl.ds(1, 2), rows],
            send_sem=xsend.at[j], recv_sem=xrecv.at[j], device_id=(t + 1, s), device_id_type=MESH,
        )

    def to_out(state, o, row):
        tile = (row - OFF) // 8
        r8 = (row - OFF) % 8
        for h in range(2):
            out[o, pl.ds(tile * TILE + r8 + 8 * h, 8, stride=16), :] = state[row, h]

    def state_out(top, hop, m, deep, act, later=0):
        at_start = (m == 0) | (deep & (m == 1))
        at_end = (m == 7) | (deep & (m == 6))
        pl.when(at_start | (at_end & end_edge))(lambda: act(edge_copy(top, hop, m, later)))
        act(main_copy(top, hop, m, later))

    no = t < 0
    hop = jnp.where(skips, 2, 1)

    def second_target(top, act):
        pl.when(forks)(lambda: each_chunk(lambda m: state_out(top, 1, m, no, act, 12)))

    def level(k, coarse_forcing, base, n):
        def emit(r, row, h, y, x):
            v[k, row, h] = y + coarse_forcing[row, h]

        step(v.at[k - 1], cc, base, n, emit)

    def span(p, n, c=0):
        return jnp.where(odd, p + (OFF + c), (OFF + MAIN - n - c) - p)

    def chain_single():
        @pl.when(z == 0)
        def _():
            def body(i, _):
                for j in range(4):
                    row = OFF - 4 + 4 * i + j
                    for h in range(2):
                        v[0, row, h] = lev[0][0, row, h]
                        v[1, row, h] = lev[COARSEN][0, row, h]
                return 0

            lax.fori_loop(0, 10, body, 0)

        later = z > 0

        def turn(i, _):
            pl.when(later & (i == 1))(lambda: arrived(1).wait_recv())
            pl.when(later & ((i < 9) | end_edge))(lambda: arrived(i + 1).wait_recv())
            pl.when(later & (i == 1))(lambda: level(1, fc.at[0], span(0, 8, -5), 8))
            pl.when(later & (i > 1))(lambda: level(1, fc.at[0], span(4 * i, 4, -5), 4))
            level(2, fc.at[1], span(4 * i, 4, -6), 4)

            @pl.when(i == 1)
            def _():
                give_forcing(0).wait_recv()
                give_forcing(1).wait_recv()

            level(3, fc.at[2], span(4 * i, 4, -7), 4)

            @pl.when(i > 1)
            def _():
                level(4, fc.at[3], span(4 * i, 4, -8), 4)
                state_out(4, hop, i - 2, skips, begin)

            return 0

        lax.fori_loop(1, 10, turn, 0)
        give_copy(2, 0, MAIN).start()
        second_target(4, begin)

    def chain_double():
        def one(j, k):
            coarse_forcing = fcx.at[k - 1] if k <= 4 else fc.at[k - 5]
            level(k, coarse_forcing, span(8 * j, 8, -8 - k), 8)

        for which in range(4):
            arrive_ahead(which)
        give_forcing(0).wait_recv()
        pl.when(z < z_last)(lambda: give_forcing(1).wait_recv())

        def turn(j, _):
            for i in range(2):
                pl.when((j < 5) | end_edge)(lambda i=i: arrived(2 * j + i).wait_recv())
            for k in (1, 2, 3):
                one(j, k)

            @pl.when(j >= 1)
            def _():
                for k in (4, 5, 6, 7):
                    one(j, k)

            @pl.when(j >= 2)
            def _():
                @pl.when(lead)
                def _():
                    one(j, 8)
                    for i in range(2):
                        state_out(8, hop, 2 * (j - 2) + i, skips, begin)

                give_copy(6, j - 2, 8).start()

            return 0

        lax.fori_loop(0, 6, turn, 0)

    def finish_first(low):
        def body(j, _):
            for r in range(8):
                row = OFF + 8 * j + r
                to_out(v.at[low], 0, row)
                to_out(v.at[low + 1], 1, row)
            return 0

        lax.fori_loop(0, 4, body, 0)

    def finish_second():
        def rows(first, n):
            for r in range(n):
                to_out(v.at[1], 0, first + r)
                to_out(v.at[2], 1, first + r)

        def body(j, _):
            pl.when(double)(lambda: give_copy(6, j, 8).wait_recv())
            rows(span(8 * j, 8), 8)
            return 0

        pl.when(single)(lambda: give_copy(2, 0, MAIN).wait_recv())
        lax.fori_loop(0, 4, body, 0)

    @pl.when((core == 0) & single)
    def _():
        chain_single()
        finish_first(0)

    @pl.when((core == 0) & double)
    def _():
        chain_double()
        finish_first(4)

    pl.when(core == 1)(finish_second)

    wait_send(near + far + near_on + far_on + fields)

    def edges_left(f, _):
        pl.when(has_dn)(lambda: edge(f, 0).wait_send())
        pl.when(has_up)(lambda: edge(f, 1).wait_send())
        return 0

    lax.fori_loop(0, n_fields, edges_left, 0)

    def drain(top):
        def body(m):
            pl.when(lead)(lambda: state_out(top, hop, m, skips, left))

        each_chunk(body)

    @pl.when((core == 0) & single)
    def _():
        drain(4)
        give_copy(2, 0, MAIN).wait_send()
        second_target(4, left)

    @pl.when((core == 0) & double)
    def _():
        drain(8)
        for j in range(4):
            give_copy(6, j, 8).wait_send()


    def forcing_left(f, _):
        pl.when(core == 1)(lambda: give_forcing(f).wait_send())
        ahead(f, left)
        pl.when(exports)(lambda: send_ahead(2, f).wait_send())
        return 0

    lax.fori_loop(0, n_fields, forcing_left, 0)


def tiles(x):
    lead = x.shape[:-2]
    n = len(lead)
    y = x.reshape(lead + (4, 8, 16, 128))
    y = y.transpose(tuple(range(n)) + (n, n + 2, n + 1, n + 3))
    return y.reshape(lead + (512, 128))


def shards(coarse_guess, initial, diffusion, velocity, reaction, source):
    hbm = pl.BlockSpec(memory_space=pltpu.HBM)
    state = (2, 8, 128)
    out = pl.pallas_call(
        kernel,
        out_shape=pltpu.VMEM((2, 512, 128), F32),
        in_specs=[hbm] * 6,
        out_specs=pl.BlockSpec(memory_space=pltpu.VMEM),
        scratch_shapes=[
            pltpu.VMEM((7, 8 * TILE, 128), F32),
            pltpu.VMEM((7, ROWS) + state, F32),
            pltpu.VMEM((7, ROWS) + state, F32),
            pltpu.VMEM((2, 2 * HALO) + state, F32),
            pltpu.VMEM((4, ROWS) + state, F32),
            pltpu.VMEM((4, ROWS) + state, F32),
            pltpu.VMEM((9, ROWS) + state, F32),
            pltpu.SemaphoreType.DMA((8,)),
            pltpu.SemaphoreType.DMA((NSEM,)),
            pltpu.SemaphoreType.DMA((NSEM,)),
            pltpu.SemaphoreType.DMA((4,)),
            pltpu.SemaphoreType.DMA((4,)),
            pltpu.SemaphoreType.DMA((24,)),
            pltpu.SemaphoreType.DMA((12,)),
            pltpu.SemaphoreType.DMA((8,)),
            pltpu.SemaphoreType.DMA((8,)),
            pltpu.SemaphoreType.DMA((10,)),
            pltpu.SemaphoreType.DMA((20,)),
            pltpu.SemaphoreType.DMA((2,)),
            pltpu.SemaphoreType.DMA((2,)),
        ] + [pltpu.VMEM((2, ROWS) + state, F32)] * (COARSEN + 1),
        compiler_params=pltpu.CompilerParams(
            collective_id=0, has_side_effects=True, vmem_limit_bytes=62 * 2**20
        ),
    )(tiles(coarse_guess), tiles(initial), tiles(diffusion), tiles(velocity), tiles(reaction), tiles(source))
    out = out.reshape(2, 4, 16, 8, 128).transpose(0, 1, 3, 2, 4)
    return out.reshape(2, 32, 2048)


def solution(mesh):
    return jax.shard_map(
        shards,
        mesh=mesh,
        in_specs=(
            P("tm", "space", None),
            P("space", None),
            P("space", None),
            P(None, "space", None),
            P("space", None),
            P("space", None),
        ),
        out_specs=P("tm", "space", None),
        check_vma=False,
    )
```
